512 devices in a mesh: sample: 16 (over z_lo, core), ctx: 32 (over x, z_hi, y).
Axes of the slice: x: 4, y: 4, z: 16 (z_hi: 2, z_lo: 8; z = z_hi * 8 + z_lo), core: 2. Of those that a mesh axis runs over, the one named last changes fastest.
Arguments:
- queries: bfloat16 [65536, 2048], P(('sample', 'ctx')), may hold values from -4 to 4
- experts: int32 [65536, 16], P(('sample', 'ctx')), may hold values from 0 to 63, all different within a row; in each aligned block of 128 rows (0 to 127, 128 to 255, ...) at most 64 rows name the same one
- gate: float32 [65536, 16], P(('sample', 'ctx')), may hold values from 0.05 to 1
- prefix_keys: bfloat16 [512, 1024], P('ctx'), may hold values from -8 to 8
- prefix_values: bfloat16 [512, 1024], P('ctx'), may hold values from -6 to 6
- d_out: bfloat16 [65536, 2048], P(('sample', 'ctx')), may hold values from -6 to 6
- lengths: int32 [64], replicated, may hold values from 128 to 1024
Outputs:
- attended: bfloat16 [65536, 2048], P(('sample', 'ctx'))
- query_grad: bfloat16 [65536, 2048], P(('sample', 'ctx'))
- gate_grad: float32 [65536, 16], P(('sample', 'ctx'))
- key_grad: float32 [512, 1024], P('ctx')
- value_grad: float32 [512, 1024], P('ctx')
The draws below stay inside these ranges and needn't reach their ends.
Inputs may be any that keep to these rules, and one draw needn't show every extreme that they name: `experts`: among the tokens of one device (aligned blocks of 128 tokens) no expert is picked more than 64 times, and some expert is picked exactly 64 times; a token's picks are distinct. Completion c holds tokens c * 1024 to (c + 1) * 1024 - 1; its first lengths[c] tokens are live.
All inputs are finite; a program needn't handle non-finite values.
Results may differ from the reference program's by a relative error of at most 0.012.
Values may be sent and summed in bfloat16 or wider, within the bound.
A program may use at most 64 MiB of HBM per device.

```python
import math
import jax
import jax.numpy as jnp
import numpy as np
from jax import lax

HEAD = 128
KV_HEADS = 8
EXPERTS = 64
TOPK = 16
CLEN = 1024
CTOK = 128
CAP = 64
TOKENS = 65536
COMPLETIONS = 64
PREFIX = 512


def draw_prefix_keys(key, part):
    base = jax.random.normal(jax.random.fold_in(key, 7), (PREFIX, KV_HEADS * HEAD), jnp.float32)
    base = jnp.clip(base, -8.0, 8.0)
    return base.astype(jnp.bfloat16)


def draw_queries(key, part):
    inner = jax.random.fold_in(key, 3)
    base = jnp.clip(jax.random.normal(inner, (TOKENS, TOPK * HEAD), jnp.float32), -4.0, 4.0)
    return base.astype(jnp.bfloat16)


def touch_ends(values, stream_key, smallest, largest):
    spot = [jax.random.randint(jax.random.fold_in(stream_key, axis), (), 0, length) for axis, length in enumerate(values.shape)]
    longest = values.shape.index(max(values.shape))
    next_to = spot[:longest] + [(spot[longest] + 1) % values.shape[longest]] + spot[longest + 1:]
    return values.at[tuple(spot)].set(smallest).at[tuple(next_to)].set(largest)


def shard_levels(key, dims, split, smallest, top_value):
    loudness, own = 1.0, jax.random.fold_in(key, 6)
    for dim, parts in split:
        steps = jnp.exp(jax.random.uniform(jax.random.fold_in(own, dim), (parts,), jnp.float32, smallest / len(split), top_value / len(split)))
        loudness = loudness * jnp.repeat(steps, dims[dim] // parts).reshape([-1 if axis == dim else 1 for axis in range(len(dims))])
    return loudness


def deal_out(own_key, own, number, rows, count, top, reach, slope):
    order = jax.random.permutation(own_key, count)
    packed, common = shares(count, rows * top, reach, slope, True), shares(count, rows * top, reach, slope, False)
    places = jnp.arange(count)

    def named(tallies, offset_by):
        used = int((tallies > 0).sum())
        fixed = max(1, used // 4)
        passed = fixed + (places - fixed + offset_by * (used - fixed)) % max(1, count - fixed)
        return jnp.zeros((count,), jnp.int32).at[order[jnp.where(places < fixed, places, passed)]].set(jnp.asarray(tallies, jnp.int32))

    tallies = jnp.where(number % 4 == 0, named(packed, number // 4), named(common, number - number // 4 - 1))
    mixed = jax.random.permutation(jax.random.fold_in(own, 3), count)
    giver, taker = mixed[0:count // 2 * 2:2], mixed[1:count // 2 * 2:2]
    slack = jnp.minimum(tallies[giver] - 1, reach - tallies[taker]) // 2
    slack = jnp.where((giver == order[0]) | (taker == order[0]) | (tallies[taker] == 0), 0, jnp.maximum(slack, 0))
    passed = jax.random.randint(jax.random.fold_in(own, 4), (count // 2,), 0, 1 << 20) % (slack + 1)
    tallies = tallies.at[giver].add(-passed).at[taker].add(passed)
    members = jnp.searchsorted(jnp.cumsum(tallies), jnp.arange(rows * top), side="right").astype(jnp.int32)
    listing = members.reshape(top, rows).T
    listing = listing[jax.random.permutation(jax.random.fold_in(own, 1), rows)]
    offset_by = jax.random.randint(jax.random.fold_in(own, 2), (rows, 1), 0, top)
    return jnp.take_along_axis(listing, (jnp.arange(top)[None, :] + offset_by) % top, axis=1)


def shares(number_of, total, most, skew, full):
    portions = [(1 << 20) // math.isqrt(grade ** skew) + 1 for grade in range(1, number_of + 1)]
    largest = most if full else min(most, max(-(-total // number_of), total * portions[0] // sum(portions)))
    least = 1 if total - largest >= number_of - 1 else 0
    given, surplus = [largest] + [least] * (number_of - 1), total - largest - least * (number_of - 1)
    while surplus > 0:
        movable = [i for i in range(1, number_of) if given[i] < largest] or [i for i in range(1, number_of) if given[i] < most]
        pool, remaining = sum([portions[i] for i in movable]), surplus
        for i in movable:
            extra = min(most - given[i], max(1, remaining * portions[i] // pool), surplus)
            given[i] = given[i] + extra
            surplus = surplus - extra
    return np.array(given)


def noise(key, shape, deviation, most, pieces=(), held_as=jnp.bfloat16):
    values = jax.random.normal(key, shape, jnp.float32) * deviation
    if len(pieces) > 0:
        values = shard_levels(key, shape, pieces, -0.22, 0.18) * values
    return jnp.clip(values, min=-most, max=most).astype(held_as)


def setup_inputs(seed: int = 0) -> dict:
    key_list = jax.random.split(jax.random.key(seed), 8)
    queries = draw_queries(jax.random.fold_in(key_list[7], 71), 0)
    experts_keys = jax.random.split(jax.random.fold_in(key_list[1], 1), TOKENS // CTOK)
    experts_turns = jax.random.permutation(jax.random.fold_in(key_list[1], 3), TOKENS // CTOK)
    experts = jax.vmap(lambda own, number: deal_out(jax.random.fold_in(key_list[1], 2), own, number, CTOK, EXPERTS, TOPK, CAP, 2))(experts_keys, experts_turns).reshape((TOKENS, TOPK))
    gate = jnp.clip(jnp.exp(math.log(1.0) - 2.9957323 * jax.random.uniform(key_list[2], (TOKENS, TOPK), jnp.float32) ** shard_levels(key_list[2], (TOKENS, TOPK), ((0, 512),), -0.2, 0.2)), 0.05, 1.0)
    prefix_keys = draw_prefix_keys(jax.random.fold_in(key_list[7], 71), 0)
    prefix_values = noise(key_list[4], (PREFIX, KV_HEADS * HEAD), 1.0, 6.0, ((0, 32),))
    d_out = noise(key_list[5], (TOKENS, TOPK * HEAD), 1.0, 6.0, ((0, 512),))
    lengths = touch_ends(jax.random.randint(key_list[6], (COMPLETIONS,), CLEN // 8, CLEN + 1), jax.random.fold_in(key_list[6], 1), CLEN // 8, CLEN).astype(jnp.int32)
    return {"queries": queries, "experts": experts, "gate": gate, "prefix_keys": prefix_keys, "prefix_values": prefix_values, "d_out": d_out, "lengths": lengths}


def slot_index(experts):
    flat = experts.reshape(-1)
    picked = (flat[:, None] == jnp.arange(EXPERTS, dtype=jnp.int32)[None, :]).astype(jnp.int32)
    before = jnp.cumsum(picked, axis=0) - picked
    return (flat * CAP + jnp.sum(before * picked, axis=1)).astype(jnp.int32)


def to_low(value):
    return lax.optimization_barrier(value.astype(jnp.bfloat16)).astype(jnp.float32)


def reference(queries, experts, gate, prefix_keys, prefix_values, d_out, lengths):
    scale = HEAD ** -0.5
    width = KV_HEADS * HEAD
    group = EXPERTS * CAP // KV_HEADS
    keys = prefix_keys.astype(jnp.float32).reshape(PREFIX, KV_HEADS, HEAD)
    values = prefix_values.astype(jnp.float32).reshape(PREFIX, KV_HEADS, HEAD)
    token_ids = jnp.arange(TOKENS, dtype=jnp.int32)
    live = (token_ids % CLEN < lengths[token_ids // CLEN]).astype(jnp.float32)
    blocks = TOKENS // CTOK

    def step(carry, item):
        q_rows, expert_rows, gate_rows, cot_rows, live_rows = item
        slots = slot_index(expert_rows)
        q_buf = jnp.zeros((EXPERTS * CAP, HEAD), jnp.bfloat16).at[slots].set(q_rows.reshape(-1, HEAD))
        q_buf = q_buf.reshape(KV_HEADS, group, HEAD).astype(jnp.float32)
        score = jnp.einsum("hgd,phd->hgp", q_buf, keys) * scale
        high = jnp.max(score, axis=2)
        weight = jnp.exp(score - high[..., None])
        total = jnp.sum(weight, axis=2)
        output = jnp.einsum("hgp,phd->hgd", to_low(weight), values) / total[..., None]
        lse = high + jnp.log(total)
        o_rows = output.reshape(EXPERTS * CAP, HEAD)[slots].reshape(CTOK, TOPK, HEAD)
        cot = cot_rows.astype(jnp.float32).reshape(CTOK, TOPK, HEAD)
        factor = gate_rows * live_rows[:, None]
        result = (factor[..., None] * o_rows).reshape(CTOK, TOPK * HEAD).astype(jnp.bfloat16)
        gate_part = live_rows[:, None] * jnp.sum(o_rows * cot, axis=2)
        dout_rows = (factor[..., None] * cot).astype(jnp.bfloat16)
        dout_buf = jnp.zeros((EXPERTS * CAP, HEAD), jnp.bfloat16).at[slots].set(dout_rows.reshape(-1, HEAD))
        dout_buf = dout_buf.reshape(KV_HEADS, group, HEAD).astype(jnp.float32)
        delta = jnp.sum(dout_buf * output, axis=2)
        prob = jnp.exp(score - lse[..., None])
        dprob = jnp.einsum("hgd,phd->hgp", dout_buf, values)
        dscore = to_low(prob * (dprob - delta[..., None]))
        dq_buf = jnp.einsum("hgp,phd->hgd", dscore, keys) * scale
        key_part = jnp.einsum("hgp,hgd->phd", dscore, q_buf) * scale
        value_part = jnp.einsum("hgp,hgd->phd", to_low(prob), dout_buf)
        dq_rows = dq_buf.reshape(EXPERTS * CAP, HEAD)[slots].reshape(CTOK, TOPK * HEAD).astype(jnp.bfloat16)
        return (carry[0] + key_part, carry[1] + value_part), (result, dq_rows, gate_part)

    items = (queries.reshape(blocks, CTOK, TOPK * HEAD), experts.reshape(blocks, CTOK, TOPK),
             gate.reshape(blocks, CTOK, TOPK), d_out.reshape(blocks, CTOK, TOPK * HEAD),
             live.reshape(blocks, CTOK))
    start = (jnp.zeros((PREFIX, KV_HEADS, HEAD), jnp.float32), jnp.zeros((PREFIX, KV_HEADS, HEAD), jnp.float32))
    sums, stacked = lax.scan(step, start, items)
    attended = stacked[0].reshape(TOKENS, TOPK * HEAD)
    query_grad = stacked[1].reshape(TOKENS, TOPK * HEAD)
    gate_grad = stacked[2].reshape(TOKENS, TOPK)
    return attended, query_grad, gate_grad, sums[0].reshape(PREFIX, width), sums[1].reshape(PREFIX, width)
```

```python
import functools
import math

import jax
import jax.numpy as jnp
from jax import lax
from jax.experimental import pallas as pl
from jax.experimental.pallas import tpu as pltpu
from jax.sharding import Mesh
from jax.sharding import PartitionSpec as P

HEAD = 128
KV_HEADS = 8
TOPK = 16
CLEN = 1024
ROWS = 128
AXES = ("zl", "core", "x", "zh", "y")
CTX = ("x", "zh", "y")
NT = (((1,), (1,)), ((), ()))
NN = (((1,), (0,)), ((), ()))
SCALE = HEAD ** (-0.5)
LOG2E = math.log2(math.e)
F32 = jnp.float32
BF16 = jnp.bfloat16
MESH = pl.DeviceIdType.MESH
VMEM = pl.BlockSpec(memory_space=pltpu.VMEM)
SMEM = pl.BlockSpec(memory_space=pltpu.SMEM)


def place():
    return tuple(lax.axis_index(a) for a in AXES)


def push(src, dst, send, recv, to):
    copy = pltpu.make_async_remote_copy(
        src_ref=src, dst_ref=dst, send_sem=send, recv_sem=recv, device_id=to, device_id_type=MESH
    )
    copy.start()
    return copy


def landed(ref, send, recv, me):
    pltpu.make_async_remote_copy(
        src_ref=ref, dst_ref=ref, send_sem=send, recv_sem=recv, device_id=me, device_id_type=MESH
    ).wait_recv()


def left(ref, send, recv, me):
    pltpu.make_async_remote_copy(
        src_ref=ref, dst_ref=ref, send_sem=send, recv_sem=recv, device_id=me, device_id_type=MESH
    ).wait_send()


def turn(i, d):
    return lax.rem(i + d, 4)


def half(core):
    return pl.ds(pl.multiple_of(core * 512, 512), 512)


def gather_kernel(kp, vp, kf, vf, ss, rs):
    zl, core, x, zh, y = place()
    me = (zl, core, x, zh, y)
    cs = half(core)
    barrier = pltpu.get_barrier_semaphore()
    edge = jnp.logical_or(zl == 0, zl == 7)
    for d in range(1, 4):
        pl.semaphore_signal(barrier, 1, device_id={"x": turn(x, d)}, device_id_type=MESH)
        pl.semaphore_signal(barrier, 1, device_id={"y": turn(y, d)}, device_id_type=MESH)
    pl.semaphore_signal(barrier, 1, device_id={"core": 1 - core}, device_id_type=MESH)
    source = jnp.where(zl < 4, 7, 0)
    pl.semaphore_signal(barrier, 1, device_id={"zh": 1 - zh, "zl": source}, device_id_type=MESH)
    pl.semaphore_wait(barrier, jnp.where(edge, 11, 7))

    def first(zr):
        ksrc = kp.at[:, cs] if zr == 0 else kf.at[1, x, y, :, cs]
        vsrc = vp.at[:, cs] if zr == 0 else vf.at[1, x, y, :, cs]
        for d in range(1, 4):
            a, b = zr * 12 + d - 1, zr * 12 + 3 + d - 1
            push(ksrc, kf.at[zr, x, y, :, cs], ss.at[a], rs.at[a], {"x": turn(x, d)})
            push(vsrc, vf.at[zr, x, y, :, cs], ss.at[b], rs.at[b], {"y": turn(y, d)})

    def second(zr):
        for d in range(1, 4):
            a = zr * 12 + d - 1
            landed(kf.at[zr, x, y, :, cs], ss.at[a], rs.at[a], me)
        for d in range(1, 4):
            a = zr * 12 + 6 + d - 1
            push(kf.at[zr, :, y, :, cs], kf.at[zr, :, y, :, cs], ss.at[a], rs.at[a], {"y": turn(y, d)})
        for d in range(1, 4):
            b = zr * 12 + 3 + d - 1
            landed(vf.at[zr, x, y, :, cs], ss.at[b], rs.at[b], me)
        for d in range(1, 4):
            b = zr * 12 + 9 + d - 1
            push(vf.at[zr, x, :, :, cs], vf.at[zr, x, :, :, cs], ss.at[b], rs.at[b], {"x": turn(x, d)})

    def third(zr):
        for d in range(1, 4):
            a = zr * 12 + 6 + d - 1
            landed(kf.at[zr, :, y, :, cs], ss.at[a], rs.at[a], me)
        push(kf.at[zr, :, :, :, cs], kf.at[zr, :, :, :, cs], ss.at[32 + zr], rs.at[32 + zr], {"core": 1 - core})
        for d in range(1, 4):
            b = zr * 12 + 9 + d - 1
            landed(vf.at[zr, x, :, :, cs], ss.at[b], rs.at[b], me)
        push(vf.at[zr, :, :, :, cs], vf.at[zr, :, :, :, cs], ss.at[34 + zr], rs.at[34 + zr], {"core": 1 - core})

    first(0)

    @pl.when(edge)
    def _():
        base = jnp.where(zl == 0, 4, 0)
        for t in range(4):
            to = {"zh": 1 - zh, "zl": base + t}
            push(kp.at[:, cs], kf.at[1, x, y, :, cs], ss.at[24 + t], rs.at[24], to)
            push(vp.at[:, cs], vf.at[1, x, y, :, cs], ss.at[28 + t], rs.at[25], to)

    kf[0, x, y, :, cs] = kp[:, cs]
    vf[0, x, y, :, cs] = vp[:, cs]
    second(0)
    landed(kf.at[1, x, y, :, cs], ss.at[24], rs.at[24], me)
    landed(vf.at[1, x, y, :, cs], ss.at[25], rs.at[25], me)
    first(1)
    third(0)
    second(1)
    third(1)
    other = half(1 - core)
    for zr in range(2):
        landed(kf.at[zr, :, :, :, other], ss.at[32 + zr], rs.at[32 + zr], me)
        landed(vf.at[zr, :, :, :, other], ss.at[34 + zr], rs.at[34 + zr], me)
    for zr in range(2):
        for d in range(1, 4):
            left(kf.at[zr, x, y, :, cs], ss.at[zr * 12 + d - 1], rs.at[0], me)
            left(vf.at[zr, x, y, :, cs], ss.at[zr * 12 + 3 + d - 1], rs.at[0], me)
            left(kf.at[zr, :, y, :, cs], ss.at[zr * 12 + 6 + d - 1], rs.at[0], me)
            left(vf.at[zr, x, :, :, cs], ss.at[zr * 12 + 9 + d - 1], rs.at[0], me)
        left(kf.at[zr, :, :, :, cs], ss.at[32 + zr], rs.at[0], me)
        left(vf.at[zr, :, :, :, cs], ss.at[34 + zr], rs.at[0], me)

    @pl.when(edge)
    def _():
        for t in range(8):
            left(kp.at[:, cs], ss.at[24 + t], rs.at[0], me)


def reduce_kernel(gv, gk, out_k, out_v, r0, p0, r1a, r1b, p1a, p1b, r2a, r2b, p2, r3, fin, ss, rs):
    zl, core, x, zh, y = place()
    me = (zl, core, x, zh, y)
    own, other = half(core), half(1 - core)
    parity, turn_z = lax.rem(zl, 2), lax.div(zl, 2)
    grads = (gv, gk)
    barrier = pltpu.get_barrier_semaphore()
    for d in range(1, 4):
        pl.semaphore_signal(barrier, 1, device_id={"x": turn(x, d)}, device_id_type=MESH)
        pl.semaphore_signal(barrier, 1, device_id={"y": turn(y, d)}, device_id_type=MESH)
    for t in range(8):
        pl.semaphore_signal(barrier, 1, device_id={"zh": 1 - zh, "zl": t}, device_id_type=MESH)
        pl.semaphore_signal(barrier, 1, device_id={"core": 1 - core, "zl": t}, device_id_type=MESH)
    for t in range(1, 8):
        pl.semaphore_signal(barrier, 1, device_id={"zl": lax.rem(zl + t, 8)}, device_id_type=MESH)
    pl.semaphore_wait(barrier, 29)

    def send0(u):
        push(grads[u].at[:, :, :, :, other], r0.at[u], ss.at[u], rs.at[u], {"core": 1 - core})

    def sum0(u):
        landed(r0.at[u], ss.at[u], rs.at[u], me)
        for zr in range(2):
            p0[u, zr] = (grads[u][zr, :, :, :, own].astype(F32) + r0[u, zr].astype(F32)).astype(BF16)

    def send1(u):
        for d in range(1, 4):
            a, b = 2 + u * 6 + d - 1, 5 + u * 6 + d - 1
            xp, yp = turn(x, d), turn(y, d)
            push(p0.at[u, :, xp, :, :, 0:256], r1a.at[u, d - 1], ss.at[a], rs.at[a], {"x": xp})
            push(p0.at[u, :, :, yp, :, 256:512], r1b.at[u, d - 1], ss.at[b], rs.at[b], {"y": yp})

    def sum1(u):
        for d in range(3):
            landed(r1a.at[u, d], ss.at[2 + u * 6 + d], rs.at[2 + u * 6 + d], me)
            landed(r1b.at[u, d], ss.at[5 + u * 6 + d], rs.at[5 + u * 6 + d], me)
        a = p0[u, :, x, :, :, 0:256].astype(F32)
        b = p0[u, :, :, y, :, 256:512].astype(F32)
        for d in range(3):
            a = a + r1a[u, d].astype(F32)
            b = b + r1b[u, d].astype(F32)
        p1a[u] = a.astype(BF16)
        p1b[u] = b.astype(BF16)

    def send2(u):
        for d in range(1, 4):
            a, b = 14 + u * 6 + d - 1, 17 + u * 6 + d - 1
            xp, yp = turn(x, d), turn(y, d)
            push(p1a.at[u, :, yp], r2a.at[u, d - 1], ss.at[a], rs.at[a], {"y": yp})
            push(p1b.at[u, :, xp], r2b.at[u, d - 1], ss.at[b], rs.at[b], {"x": xp})

    def sum2(u):
        for d in range(3):
            landed(r2a.at[u, d], ss.at[14 + u * 6 + d], rs.at[14 + u * 6 + d], me)
            landed(r2b.at[u, d], ss.at[17 + u * 6 + d], rs.at[17 + u * 6 + d], me)
        a = p1a[u, :, y].astype(F32)
        b = p1b[u, :, x].astype(F32)
        for d in range(3):
            a = a + r2a[u, d].astype(F32)
            b = b + r2b[u, d].astype(F32)
        for j in range(2):
            p2[u, :, j] = a[:, :, j * 128 : (j + 1) * 128].astype(BF16)
            p2[u, :, 2 + j] = b[:, :, j * 128 : (j + 1) * 128].astype(BF16)

    def send3(u):
        for zr in range(2):
            zt = zh if zr == 0 else 1 - zh
            for j in range(4):
                at = 26 + u * 8 + zr * 4 + j

                def go(zr=zr, zt=zt, j=j, at=at):
                    push(p2.at[u, zr, j], r3.at[zr, zl], ss.at[at], rs.at[26 + zr * 8 + zl], {"zh": zt, "zl": 2 * j + u})

                if zr == 0:
                    pl.when(zl != 2 * j + u)(go)
                else:
                    go()

    def sum3(u):
        @pl.when(parity == u)
        def _():
            for zr in range(2):
                for t in range(8):
                    def get(zr=zr, t=t):
                        landed(r3.at[zr, t], ss.at[26], rs.at[26 + zr * 8 + t], me)

                    if zr == 0:
                        pl.when(zl != t)(get)
                    else:
                        get()
            r3[0, zl] = p2[u, 0, turn_z]
            acc = r3[0, 0].astype(F32)
            for i in range(1, 16):
                acc = acc + r3[i // 8, i % 8].astype(F32)
            fin[u, core, turn_z] = acc.astype(BF16)
            for c in range(2):
                for t in range(8):
                    def go(c=c, t=t):
                        push(
                            fin.at[u, core, turn_z], fin.at[u, core, turn_z], ss.at[42 + c * 8 + t],
                            rs.at[42 + u * 8 + core * 4 + turn_z], {"core": c, "zl": t},
                        )

                    pl.when(jnp.logical_or(core != c, zl != t))(go)

    def finish(u, out):
        for c in range(2):
            for j in range(4):
                @pl.when(jnp.logical_or(core != c, zl != 2 * j + u))
                def _(c=c, j=j):
                    landed(fin.at[u, c, j], ss.at[42], rs.at[42 + u * 8 + c * 4 + j], me)

                out[:, (c * 4 + j) * 128 : (c * 4 + j + 1) * 128] = fin[u, c, j].astype(F32)

    for u in range(2):
        send0(u)
    for u in range(2):
        sum0(u)
        send1(u)
    for u in range(2):
        sum1(u)
        send2(u)
    for u in range(2):
        sum2(u)
        send3(u)
    for u in range(2):
        sum3(u)
    finish(0, out_v)
    finish(1, out_k)
    for u in range(2):
        left(r0.at[u], ss.at[u], rs.at[0], me)
        for d in range(3):
            left(r1a.at[u, d], ss.at[2 + u * 6 + d], rs.at[0], me)
            left(r1b.at[u, d], ss.at[5 + u * 6 + d], rs.at[0], me)
            left(r2a.at[u, d], ss.at[14 + u * 6 + d], rs.at[0], me)
            left(r2b.at[u, d], ss.at[17 + u * 6 + d], rs.at[0], me)
        for zr in range(2):
            for j in range(4):
                def done(u=u, zr=zr, j=j):
                    left(p2.at[u, zr, j], ss.at[26 + u * 8 + zr * 4 + j], rs.at[0], me)

                if zr == 0:
                    pl.when(zl != 2 * j + u)(done)
                else:
                    done()
    for c in range(2):
        for t in range(8):
            @pl.when(jnp.logical_or(core != c, zl != t))
            def _(c=c, t=t):
                left(fin.at[0, 0, 0], ss.at[42 + c * 8 + t], rs.at[0], me)


def compute_kernel(len_ref, eT, gT, q, do, k, v, att, dq, ggT, dk, dv, qx, dx, pf, ds, vt, kt):
    zl, core, x, zh, y = place()
    block = ((zl * 2 + core) * 32) + ((x * 2 + zh) * 4 + y)
    per = CLEN // ROWS
    length = len_ref[lax.div(block, per)]
    token = lax.broadcasted_iota(jnp.int32, (1, ROWS), 1) + lax.rem(block, per) * ROWS
    live = (token < length).astype(F32)
    headT = lax.div(eT[...], 8)
    for p in range(TOPK):
        rows = slice(p * 128, (p + 1) * 128)
        hc = jnp.transpose(jnp.broadcast_to(headT[p : p + 1, :].astype(F32), (128, 128)))
        q32 = q[:, rows].astype(F32)
        d32 = do[:, rows].astype(F32)
        for h in range(KV_HEADS):
            mine = hc == float(h)
            cols = slice(h * 128, (h + 1) * 128)
            qx[rows, cols] = jnp.where(mine, q32, 0.0).astype(BF16)
            dx[rows, cols] = jnp.where(mine, d32, 0.0).astype(BF16)
    lv = jnp.concatenate([live, live], axis=1)
    for kk in range(8):
        rows = pl.ds(kk * 256, 256)
        s = lax.dot_general(k[...], qx[rows, :], NT, preferred_element_type=F32)
        dp = lax.dot_general(v[...], dx[rows, :], NT, preferred_element_type=F32)
        m = jnp.max(s, axis=0, keepdims=True)
        e = jnp.exp2((s - m) * (SCALE * LOG2E))
        inv = 1.0 / jnp.sum(e, axis=0, keepdims=True)
        g = jnp.sum(e * dp, axis=0, keepdims=True) * inv
        gate = jnp.concatenate([gT[2 * kk : 2 * kk + 1, :], gT[2 * kk + 1 : 2 * kk + 2, :]], axis=1)
        w = e * (gate * lv * inv)
        pf[:, rows] = w.astype(BF16)
        ds[:, rows] = (w * (dp - g)).astype(BF16)
        gg = g * lv
        ggT[2 * kk : 2 * kk + 1, :] = gg[:, :128]
        ggT[2 * kk + 1 : 2 * kk + 2, :] = gg[:, 128:]
    for c in range(4):
        cols = pl.ds(c * 256, 256)
        dv[:, cols] = lax.dot_general(pf[...], dx[:, cols], NN, preferred_element_type=F32).astype(BF16)
    for c in range(4):
        cols = pl.ds(c * 256, 256)
        dk[:, cols] = (lax.dot_general(ds[...], qx[:, cols], NN, preferred_element_type=F32) * SCALE).astype(BF16)
    vt[...] = jnp.transpose(v[...])
    kt[...] = jnp.transpose(k[...])
    for src, mat, out, by in ((pf, vt, att, 1.0), (ds, kt, dq, SCALE)):
        for kk in range(8):
            hd = jnp.concatenate([headT[2 * kk : 2 * kk + 1, :], headT[2 * kk + 1 : 2 * kk + 2, :]], axis=1)
            full = lax.dot_general(mat[...], src[:, kk * 256 : (kk + 1) * 256], NN, preferred_element_type=F32)
            acc = full[:128, :]
            for h in range(1, KV_HEADS):
                acc = jnp.where(hd == h, full[h * 128 : (h + 1) * 128, :], acc)
            acc = acc * by
            for j in range(2):
                at = (2 * kk + j) * 128
                out[:, at : at + 128] = jnp.transpose(acc[:, j * 128 : (j + 1) * 128]).astype(BF16)


def local(queries, experts, gate, prefix_keys, prefix_values, d_out, lengths):
    full = jax.ShapeDtypeStruct((2, 4, 4, 16, 1024), BF16)
    kf, vf = pl.pallas_call(
        gather_kernel,
        out_shape=(full, full),
        in_specs=[VMEM] * 2,
        out_specs=(VMEM,) * 2,
        scratch_shapes=[pltpu.SemaphoreType.DMA((36,)), pltpu.SemaphoreType.DMA((36,))],
        compiler_params=pltpu.CompilerParams(collective_id=0, has_side_effects=True, vmem_limit_bytes=16 << 20),
        name="gather",
    )(prefix_keys, prefix_values)
    rows = jax.ShapeDtypeStruct((ROWS, TOPK * HEAD), BF16)
    grad = jax.ShapeDtypeStruct((512, 1024), BF16)
    att, dq, ggT, dk, dv = pl.pallas_call(
        compute_kernel,
        out_shape=(rows, rows, jax.ShapeDtypeStruct((TOPK, ROWS), F32), grad, grad),
        in_specs=[SMEM] + [VMEM] * 6,
        out_specs=(VMEM,) * 5,
        scratch_shapes=[
            pltpu.VMEM((2048, 1024), BF16),
            pltpu.VMEM((2048, 1024), BF16),
            pltpu.VMEM((512, 2048), BF16),
            pltpu.VMEM((512, 2048), BF16),
            pltpu.VMEM((1024, 512), BF16),
            pltpu.VMEM((1024, 512), BF16),
        ],
        compiler_params=pltpu.CompilerParams(vmem_limit_bytes=56 << 20),
        name="attention",
    )(lengths, experts.T, gate.T, queries, d_out, kf.reshape(512, 1024), vf.reshape(512, 1024))
    owned = jax.ShapeDtypeStruct((16, 1024), F32)
    key_grad, value_grad = pl.pallas_call(
        reduce_kernel,
        out_shape=(owned, owned),
        in_specs=[VMEM] * 2,
        out_specs=(VMEM,) * 2,
        scratch_shapes=[
            pltpu.VMEM((2, 2, 4, 4, 16, 512), BF16),
            pltpu.VMEM((2, 2, 4, 4, 16, 512), BF16),
            pltpu.VMEM((2, 3, 2, 4, 16, 256), BF16),
            pltpu.VMEM((2, 3, 2, 4, 16, 256), BF16),
            pltpu.VMEM((2, 2, 4, 16, 256), BF16),
            pltpu.VMEM((2, 2, 4, 16, 256), BF16),
            pltpu.VMEM((2, 3, 2, 16, 256), BF16),
            pltpu.VMEM((2, 3, 2, 16, 256), BF16),
            pltpu.VMEM((2, 2, 4, 16, 128), BF16),
            pltpu.VMEM((2, 8, 16, 128), BF16),
            pltpu.VMEM((2, 2, 4, 16, 128), BF16),
            pltpu.SemaphoreType.DMA((58,)),
            pltpu.SemaphoreType.DMA((58,)),
        ],
        compiler_params=pltpu.CompilerParams(collective_id=1, has_side_effects=True, vmem_limit_bytes=32 << 20),
        name="reduce",
    )(dv.reshape(2, 4, 4, 16, 1024), dk.reshape(2, 4, 4, 16, 1024))
    return att, dq, ggT.T, key_grad, value_grad


def solution(mesh):
    torus = Mesh(mesh.devices.reshape(8, 2, 4, 2, 4), AXES)
    in_specs = (P(AXES, None), P(AXES, None), P(AXES, None), P(CTX, None), P(CTX, None), P(AXES, None), P())
    out_specs = (P(AXES, None), P(AXES, None), P(AXES, None), P(CTX, None), P(CTX, None))
    return jax.shard_map(local, mesh=torus, in_specs=in_specs, out_specs=out_specs, check_vma=False)
```

```python
import functools
import math

import jax
import jax.numpy as jnp
from jax import lax
from jax.experimental import pallas as pl
from jax.experimental.pallas import tpu as pltpu
from jax.sharding import Mesh
from jax.sharding import PartitionSpec as P

HEAD = 128
KV_HEADS = 8
TOPK = 16
CLEN = 1024
ROWS = 128
AXES = ("zl", "core", "x", "zh", "y")
CTX = ("x", "zh", "y")
NT = (((1,), (1,)), ((), ()))
NN = (((1,), (0,)), ((), ()))
SCALE = HEAD ** (-0.5)
LOG2E = math.log2(math.e)
F32 = jnp.float32
BF16 = jnp.bfloat16
MESH = pl.DeviceIdType.MESH
VMEM = pl.BlockSpec(memory_space=pltpu.VMEM)
SMEM = pl.BlockSpec(memory_space=pltpu.SMEM)


def place():
    return tuple(lax.axis_index(a) for a in AXES)


def push(src, dst, send, recv, to):
    copy = pltpu.make_async_remote_copy(
        src_ref=src, dst_ref=dst, send_sem=send, recv_sem=recv, device_id=to, device_id_type=MESH
    )
    copy.start()
    return copy


def landed(ref, send, recv, me):
    pltpu.make_async_remote_copy(
        src_ref=ref, dst_ref=ref, send_sem=send, recv_sem=recv, device_id=me, device_id_type=MESH
    ).wait_recv()


def left(ref, send, recv, me):
    pltpu.make_async_remote_copy(
        src_ref=ref, dst_ref=ref, send_sem=send, recv_sem=recv, device_id=me, device_id_type=MESH
    ).wait_send()


def turn(i, d):
    return lax.rem(i + d, 4)


def half(core):
    return pl.ds(pl.multiple_of(core * 512, 512), 512)


def kernel(
    len_ref, eT_in, gT_in, q_in, d_in, kp, vp,
    att, dq, ggT, out_k, out_v,
    eT, gT, q, do, kf, vf, qx, dx, s0, d0, pf, ds, vt, kt,
    far, near, r0, p0, r1, p1, r2, p2, r3, fin, ls, gs, gr, ss, rs,
):
    zl, core, x, zh, y = place()
    me = (zl, core, x, zh, y)
    cs, other = half(core), half(1 - core)
    parity, turn_z = lax.rem(zl, 2), lax.div(zl, 2)
    edge = jnp.logical_or(zl == 0, zl == 7)

    loads = [
        pltpu.make_async_copy(kp.at[:, cs], kf.at[0, x, y, :, cs], ls.at[0]),
        pltpu.make_async_copy(vp.at[:, cs], vf.at[0, x, y, :, cs], ls.at[1]),
        pltpu.make_async_copy(eT_in, eT, ls.at[2]),
        pltpu.make_async_copy(gT_in, gT, ls.at[3]),
        pltpu.make_async_copy(q_in, q, ls.at[4]),
        pltpu.make_async_copy(d_in, do, ls.at[5]),
    ]
    for c in loads:
        c.start()

    barrier = pltpu.get_barrier_semaphore()
    for d in range(1, 4):
        pl.semaphore_signal(barrier, 1, device_id={"x": turn(x, d)}, device_id_type=MESH)
        pl.semaphore_signal(barrier, 1, device_id={"y": turn(y, d)}, device_id_type=MESH)
    for t in range(8):
        pl.semaphore_signal(barrier, 1, device_id={"zh": 1 - zh, "zl": t}, device_id_type=MESH)
        pl.semaphore_signal(barrier, 1, device_id={"core": 1 - core, "zl": t}, device_id_type=MESH)
    for t in range(1, 8):
        pl.semaphore_signal(barrier, 1, device_id={"zl": lax.rem(zl + t, 8)}, device_id_type=MESH)

    for c in loads[2:]:
        c.wait()
    headT = lax.div(eT[...], 8)
    for p in range(TOPK):
        rows = slice(p * 128, (p + 1) * 128)
        hc = jnp.transpose(jnp.broadcast_to(headT[p : p + 1, :].astype(F32), (128, 128)))
        q32 = q[:, rows].astype(F32)
        d32 = do[:, rows].astype(F32)
        for h in range(KV_HEADS):
            mine = hc == float(h)
            cols = slice(h * 128, (h + 1) * 128)
            qx[rows, cols] = jnp.where(mine, q32, 0.0).astype(BF16)
            dx[rows, cols] = jnp.where(mine, d32, 0.0).astype(BF16)
    for c in loads[:2]:
        c.wait()
    pl.semaphore_wait(barrier, 29)

    def gpush(src, dst, at, to):
        push(src, dst, gs.at[at], gr.at[at], to)

    def glanded(ref, at):
        landed(ref, gs.at[at], gr.at[at], me)

    def first(zr):
        for d in range(1, 4):
            a, b = zr * 12 + d - 1, zr * 12 + 3 + d - 1
            gpush(kf.at[zr, x, y, :, cs], kf.at[zr, x, y, :, cs], a, {"x": turn(x, d)})
            gpush(vf.at[zr, x, y, :, cs], vf.at[zr, x, y, :, cs], b, {"y": turn(y, d)})

    def second(zr):
        for d in range(3):
            glanded(kf.at[zr, x, y, :, cs], zr * 12 + d)
        for d in range(1, 4):
            gpush(kf.at[zr, :, y, :, cs], kf.at[zr, :, y, :, cs], zr * 12 + 6 + d - 1, {"y": turn(y, d)})
        for d in range(3):
            glanded(vf.at[zr, x, y, :, cs], zr * 12 + 3 + d)
        for d in range(1, 4):
            gpush(vf.at[zr, x, :, :, cs], vf.at[zr, x, :, :, cs], zr * 12 + 9 + d - 1, {"x": turn(x, d)})

    def third(zr):
        for d in range(3):
            glanded(kf.at[zr, :, y, :, cs], zr * 12 + 6 + d)
        gpush(kf.at[zr, :, :, :, cs], kf.at[zr, :, :, :, cs], 32 + zr, {"core": 1 - core})
        for d in range(3):
            glanded(vf.at[zr, x, :, :, cs], zr * 12 + 9 + d)
        gpush(vf.at[zr, :, :, :, cs], vf.at[zr, :, :, :, cs], 34 + zr, {"core": 1 - core})

    def swapped(zr):
        glanded(kf.at[zr, :, :, :, other], 32 + zr)
        glanded(vf.at[zr, :, :, :, other], 34 + zr)

    @pl.when(edge)
    def _():
        base = jnp.where(zl == 0, 4, 0)
        for t in range(4):
            to = {"zh": 1 - zh, "zl": base + t}
            push(kf.at[0, x, y, :, cs], kf.at[1, x, y, :, cs], gs.at[24 + t], gr.at[24], to)
            push(vf.at[0, x, y, :, cs], vf.at[1, x, y, :, cs], gs.at[28 + t], gr.at[25], to)

    first(0)
    second(0)
    glanded(kf.at[1, x, y, :, cs], 24)
    glanded(vf.at[1, x, y, :, cs], 25)
    first(1)
    third(0)
    second(1)
    swapped(0)
    k0, v0 = kf[0].reshape(256, 1024), vf[0].reshape(256, 1024)
    for kk in range(8):
        rows = pl.ds(kk * 256, 256)
        s0[:, rows] = lax.dot_general(k0, qx[rows, :], NT, preferred_element_type=F32)
        d0[:, rows] = lax.dot_general(v0, dx[rows, :], NT, preferred_element_type=F32)
    third(1)
    swapped(1)

    block = ((zl * 2 + core) * 32) + ((x * 2 + zh) * 4 + y)
    per = CLEN // ROWS
    length = len_ref[lax.div(block, per)]
    token = lax.broadcasted_iota(jnp.int32, (1, ROWS), 1) + lax.rem(block, per) * ROWS
    live = (token < length).astype(F32)
    lv = jnp.concatenate([live, live], axis=1)
    k1, v1 = kf[1].reshape(256, 1024), vf[1].reshape(256, 1024)
    for kk in range(8):
        rows = pl.ds(kk * 256, 256)
        s = jnp.concatenate(
            [s0[:, rows], lax.dot_general(k1, qx[rows, :], NT, preferred_element_type=F32)], axis=0
        )
        dp = jnp.concatenate(
            [d0[:, rows], lax.dot_general(v1, dx[rows, :], NT, preferred_element_type=F32)], axis=0
        )
        m = jnp.max(s, axis=0, keepdims=True)
        e = jnp.exp2((s - m) * (SCALE * LOG2E))
        inv = 1.0 / jnp.sum(e, axis=0, keepdims=True)
        g = jnp.sum(e * dp, axis=0, keepdims=True) * inv
        gate = jnp.concatenate([gT[2 * kk : 2 * kk + 1, :], gT[2 * kk + 1 : 2 * kk + 2, :]], axis=1)
        w = e * (gate * lv * inv)
        pf[:, rows] = w.astype(BF16)
        ds[:, rows] = (w * (dp - g)).astype(BF16)
        gg = g * lv
        ggT[2 * kk : 2 * kk + 1, :] = gg[:, :128]
        ggT[2 * kk + 1 : 2 * kk + 2, :] = gg[:, 128:]

    def product(u, base, n):
        left_side, right_side = ((pf, dx), (ds, qx))[u]
        cols = pl.ds(pl.multiple_of(base * 512 + n * 256, 256), 256)
        made = lax.dot_general(left_side[...], right_side[:, cols], NN, preferred_element_type=F32)
        if u == 1:
            made = made * SCALE
        return made.reshape(2, 4, 4, 16, 256)

    def send0(u, n):
        far[u, n] = product(u, 1 - core, n).astype(BF16)
        at = u * 2 + n
        push(far.at[u, n], r0.at[u, n], ss.at[at], rs.at[at], {"core": 1 - core})

    def send1(u, n):
        near[...] = product(u, core, n)
        at = u * 2 + n
        landed(r0.at[u, n], ss.at[at], rs.at[at], me)
        p0[u, n] = (near[...] + r0[u, n].astype(F32)).astype(BF16)
        for d in range(1, 4):
            at = 4 + (u * 2 + n) * 3 + d - 1
            if n == 0:
                xp = turn(x, d)
                push(p0.at[u, n, :, xp], r1.at[u, n, d - 1], ss.at[at], rs.at[at], {"x": xp})
            else:
                yp = turn(y, d)
                push(p0.at[u, n, :, :, yp], r1.at[u, n, d - 1], ss.at[at], rs.at[at], {"y": yp})

    def send2(u):
        for n in range(2):
            for d in range(3):
                at = 4 + (u * 2 + n) * 3 + d
                landed(r1.at[u, n, d], ss.at[at], rs.at[at], me)
            own = p0[u, n, :, x] if n == 0 else p0[u, n, :, :, y]
            acc = own.astype(F32)
            for d in range(3):
                acc = acc + r1[u, n, d].astype(F32)
            p1[u, n] = acc.astype(BF16)
            for d in range(1, 4):
                at = 16 + (u * 2 + n) * 3 + d - 1
                if n == 0:
                    yp = turn(y, d)
                    push(p1.at[u, n, :, yp], r2.at[u, n, d - 1], ss.at[at], rs.at[at], {"y": yp})
                else:
                    xp = turn(x, d)
                    push(p1.at[u, n, :, xp], r2.at[u, n, d - 1], ss.at[at], rs.at[at], {"x": xp})

    def send3(u):
        for n in range(2):
            for d in range(3):
                at = 16 + (u * 2 + n) * 3 + d
                landed(r2.at[u, n, d], ss.at[at], rs.at[at], me)
            own = p1[u, n, :, y] if n == 0 else p1[u, n, :, x]
            acc = own.astype(F32)
            for d in range(3):
                acc = acc + r2[u, n, d].astype(F32)
            for j in range(2):
                p2[u, :, 2 * n + j] = acc[:, :, j * 128 : (j + 1) * 128].astype(BF16)
        for zr in range(2):
            zt = zh if zr == 0 else 1 - zh
            for j in range(4):
                at = 28 + u * 8 + zr * 4 + j

                def go(zr=zr, zt=zt, j=j, at=at):
                    push(
                        p2.at[u, zr, j], r3.at[zr, zl], ss.at[at], rs.at[28 + zr * 8 + zl],
                        {"zh": zt, "zl": 2 * j + u},
                    )

                if zr == 0:
                    pl.when(zl != 2 * j + u)(go)
                else:
                    go()

    def send4(u):
        @pl.when(parity == u)
        def _():
            for zr in range(2):
                for t in range(8):
                    def get(zr=zr, t=t):
                        landed(r3.at[zr, t], ss.at[28], rs.at[28 + zr * 8 + t], me)

                    if zr == 0:
                        pl.when(zl != t)(get)
                    else:
                        get()
            r3[0, zl] = p2[u, 0, turn_z]
            acc = r3[0, 0].astype(F32)
            for i in range(1, 16):
                acc = acc + r3[i // 8, i % 8].astype(F32)
            fin[u, core, turn_z] = acc.astype(BF16)
            for c in range(2):
                for t in range(8):
                    def go(c=c, t=t):
                        push(
                            fin.at[u, core, turn_z], fin.at[u, core, turn_z], ss.at[44 + c * 8 + t],
                            rs.at[44 + u * 8 + core * 4 + turn_z], {"core": c, "zl": t},
                        )

                    pl.when(jnp.logical_or(core != c, zl != t))(go)

    def finish(u, out):
        for c in range(2):
            for j in range(4):
                @pl.when(jnp.logical_or(core != c, zl != 2 * j + u))
                def _(c=c, j=j):
                    landed(fin.at[u, c, j], ss.at[44], rs.at[44 + u * 8 + c * 4 + j], me)

                out[:, (c * 4 + j) * 128 : (c * 4 + j + 1) * 128] = fin[u, c, j].astype(F32)

    def rows_out(src, mat, out, by):
        for kk in range(8):
            hd = jnp.concatenate([headT[2 * kk : 2 * kk + 1, :], headT[2 * kk + 1 : 2 * kk + 2, :]], axis=1)
            full = lax.dot_general(mat[...], src[:, kk * 256 : (kk + 1) * 256], NN, preferred_element_type=F32)
            acc = full[:128, :]
            for h in range(1, KV_HEADS):
                acc = jnp.where(hd == h, full[h * 128 : (h + 1) * 128, :], acc)
            acc = acc * by
            for j in range(2):
                at = (2 * kk + j) * 128
                out[:, at : at + 128] = jnp.transpose(acc[:, j * 128 : (j + 1) * 128]).astype(BF16)

    for u in range(2):
        send0(u, 0)
        send0(u, 1)
        send1(u, 0)
        send1(u, 1)
    send2(0)
    send2(1)
    send3(0)
    send3(1)
    vt[...] = jnp.transpose(vf[...].reshape(512, 1024))
    rows_out(pf, vt, att, 1.0)
    send4(0)
    kt[...] = jnp.transpose(kf[...].reshape(512, 1024))
    rows_out(ds, kt, dq, SCALE)
    send4(1)
    finish(0, out_v)
    finish(1, out_k)

    for zr in range(2):
        for d in range(3):
            left(kf.at[zr, x, y, :, cs], gs.at[zr * 12 + d], gr.at[0], me)
            left(vf.at[zr, x, y, :, cs], gs.at[zr * 12 + 3 + d], gr.at[0], me)
            left(kf.at[zr, :, y, :, cs], gs.at[zr * 12 + 6 + d], gr.at[0], me)
            left(vf.at[zr, x, :, :, cs], gs.at[zr * 12 + 9 + d], gr.at[0], me)
        left(kf.at[zr, :, :, :, cs], gs.at[32 + zr], gr.at[0], me)
        left(vf.at[zr, :, :, :, cs], gs.at[34 + zr], gr.at[0], me)

    @pl.when(edge)
    def _():
        for t in range(8):
            left(kf.at[0, x, y, :, cs], gs.at[24 + t], gr.at[0], me)

    for u in range(2):
        for n in range(2):
            left(far.at[u, n], ss.at[u * 2 + n], rs.at[0], me)
            for d in range(3):
                left(r1.at[u, n, d], ss.at[4 + (u * 2 + n) * 3 + d], rs.at[0], me)
                left(r2.at[u, n, d], ss.at[16 + (u * 2 + n) * 3 + d], rs.at[0], me)
        for zr in range(2):
            for j in range(4):
                def done(u=u, zr=zr, j=j):
                    left(p2.at[u, zr, j], ss.at[28 + u * 8 + zr * 4 + j], rs.at[0], me)

                if zr == 0:
                    pl.when(zl != 2 * j + u)(done)
                else:
                    done()
    for c in range(2):
        for t in range(8):
            @pl.when(jnp.logical_or(core != c, zl != t))
            def _(c=c, t=t):
                left(fin.at[0, 0, 0], ss.at[44 + c * 8 + t], rs.at[0], me)


def local(queries, experts, gate, prefix_keys, prefix_values, d_out, lengths):
    rows = jax.ShapeDtypeStruct((ROWS, TOPK * HEAD), BF16)
    owned = jax.ShapeDtypeStruct((16, 1024), F32)
    HBM = pl.BlockSpec(memory_space=pl.ANY)
    full = pltpu.VMEM((2, 4, 4, 16, 1024), BF16)
    att, dq, ggT, key_grad, value_grad = pl.pallas_call(
        kernel,
        out_shape=(rows, rows, jax.ShapeDtypeStruct((TOPK, ROWS), F32), owned, owned),
        in_specs=[SMEM] + [HBM] * 6,
        out_specs=(VMEM,) * 5,
        scratch_shapes=[
            pltpu.VMEM((TOPK, ROWS), jnp.int32),
            pltpu.VMEM((TOPK, ROWS), F32),
            pltpu.VMEM((ROWS, 2048), BF16),
            pltpu.VMEM((ROWS, 2048), BF16),
            full,
            full,
            pltpu.VMEM((2048, 1024), BF16),
            pltpu.VMEM((2048, 1024), BF16),
            pltpu.VMEM((256, 2048), F32),
            pltpu.VMEM((256, 2048), F32),
            pltpu.VMEM((512, 2048), BF16),
            pltpu.VMEM((512, 2048), BF16),
            pltpu.VMEM((1024, 512), BF16),
            pltpu.VMEM((1024, 512), BF16),
            pltpu.VMEM((2, 2, 2, 4, 4, 16, 256), BF16),
            pltpu.VMEM((2, 4, 4, 16, 256), F32),
            pltpu.VMEM((2, 2, 2, 4, 4, 16, 256), BF16),
            pltpu.VMEM((2, 2, 2, 4, 4, 16, 256), BF16),
            pltpu.VMEM((2, 2, 3, 2, 4, 16, 256), BF16),
            pltpu.VMEM((2, 2, 2, 4, 16, 256), BF16),
            pltpu.VMEM((2, 2, 3, 2, 16, 256), BF16),
            pltpu.VMEM((2, 2, 4, 16, 128), BF16),
            pltpu.VMEM((2, 8, 16, 128), BF16),
            pltpu.VMEM((2, 2, 4, 16, 128), BF16),
            pltpu.SemaphoreType.DMA((6,)),
            pltpu.SemaphoreType.DMA((36,)),
            pltpu.SemaphoreType.DMA((36,)),
            pltpu.SemaphoreType.DMA((60,)),
            pltpu.SemaphoreType.DMA((60,)),
        ],
        compiler_params=pltpu.CompilerParams(collective_id=0, has_side_effects=True, vmem_limit_bytes=60 << 20),
        name="prefix",
    )(lengths, experts.T, gate.T, queries, d_out, prefix_keys, prefix_values)
    return att, dq, ggT.T, key_grad, value_grad


def solution(mesh):
    torus = Mesh(mesh.devices.reshape(8, 2, 4, 2, 4), AXES)
    in_specs = (P(AXES, None), P(AXES, None), P(AXES, None), P(CTX, None), P(CTX, None), P(AXES, None), P())
    out_specs = (P(AXES, None), P(AXES, None), P(AXES, None), P(CTX, None), P(CTX, None))
    return jax.shard_map(local, mesh=torus, in_specs=in_specs, out_specs=out_specs, check_vma=False)
```

```python
import functools
import math

import jax
import jax.numpy as jnp
from jax import lax
from jax.experimental import pallas as pl
from jax.experimental.pallas import tpu as pltpu
from jax.sharding import Mesh
from jax.sharding import PartitionSpec as P

HEAD = 128
KV_HEADS = 8
TOPK = 16
CLEN = 1024
ROWS = 128
AXES = ("zl", "core", "x", "zh", "y")
CTX = ("x", "zh", "y")
NT = (((1,), (1,)), ((), ()))
NN = (((1,), (0,)), ((), ()))
SCALE = HEAD ** (-0.5)
LOG2E = math.log2(math.e)
F32 = jnp.float32
BF16 = jnp.bfloat16
MESH = pl.DeviceIdType.MESH
VMEM = pl.BlockSpec(memory_space=pltpu.VMEM)
SMEM = pl.BlockSpec(memory_space=pltpu.SMEM)


def place():
    return tuple(lax.axis_index(a) for a in AXES)


def push(src, dst, send, recv, to):
    copy = pltpu.make_async_remote_copy(
        src_ref=src, dst_ref=dst, send_sem=send, recv_sem=recv, device_id=to, device_id_type=MESH
    )
    copy.start()
    return copy


def landed(ref, send, recv, me):
    pltpu.make_async_remote_copy(
        src_ref=ref, dst_ref=ref, send_sem=send, recv_sem=recv, device_id=me, device_id_type=MESH
    ).wait_recv()


def left(ref, send, recv, me):
    pltpu.make_async_remote_copy(
        src_ref=ref, dst_ref=ref, send_sem=send, recv_sem=recv, device_id=me, device_id_type=MESH
    ).wait_send()


def turn(i, d):
    return lax.rem(i + d, 4)


def half(core):
    return pl.ds(pl.multiple_of(core * 512, 512), 512)


def kernel(
    len_in, eT_in, gT_in, q_in, d_in, kp, vp,
    att, dq, ggT, out_k, out_v,
    len_ref, eT, gT, q, do, kf, vf, qx, dx, s0, d0, pf, ds, vt, kt,
    far, near, r0, p0, r1, p1, r2, p2, r3, fin, ls, gs, gr, ss, rs, known, both,
):
    zl, core, x, zh, y = place()
    me = (zl, core, x, zh, y)
    cs, other = half(core), half(1 - core)
    owner, mine_j = jnp.logical_and(zl >= 2, zl < 6), jnp.clip(zl - 2, 0, 3)
    edge = jnp.logical_or(zl == 0, zl == 7)

    loads = [
        pltpu.make_async_copy(kp.at[:, cs], kf.at[0, x, y, :, cs], ls.at[0]),
        pltpu.make_async_copy(vp.at[:, cs], vf.at[0, x, y, :, cs], ls.at[1]),
        pltpu.make_async_copy(eT_in, eT, ls.at[2]),
        pltpu.make_async_copy(gT_in, gT, ls.at[3]),
        pltpu.make_async_copy(q_in, q, ls.at[4]),
        pltpu.make_async_copy(d_in, do, ls.at[5]),
        pltpu.make_async_copy(len_in, len_ref, ls.at[6]),
    ]
    for c in loads:
        c.start()

    def along_z(d):
        z = lax.rem(zh * 8 + zl + d, 16)
        return {"zh": lax.div(z, 8), "zl": lax.rem(z, 8)}

    barrier = pltpu.get_barrier_semaphore()
    for d in range(1, 4):
        pl.semaphore_signal(barrier, 1, device_id={"x": turn(x, d)}, device_id_type=MESH)
        pl.semaphore_signal(barrier, 1, device_id={"y": turn(y, d)}, device_id_type=MESH)
    pl.semaphore_signal(barrier, 1, device_id={"core": 1 - core}, device_id_type=MESH)
    for d in (1, 2, 3, 4, 12, 13, 14, 15):
        pl.semaphore_signal(barrier, 1, device_id=along_z(d), device_id_type=MESH)
    pl.semaphore_wait(barrier, 15)

    def gpush(src, dst, at, to):
        push(src, dst, gs.at[at], gr.at[at], to)

    def glanded(ref, at):
        landed(ref, gs.at[at], gr.at[at], me)

    def first(zr):
        for d in range(1, 4):
            a, b = zr * 12 + d - 1, zr * 12 + 3 + d - 1
            gpush(kp.at[:, cs] if zr == 0 else kf.at[1, x, y, :, cs], kf.at[zr, x, y, :, cs], a, {"x": turn(x, d)})
            gpush(vp.at[:, cs] if zr == 0 else vf.at[1, x, y, :, cs], vf.at[zr, x, y, :, cs], b, {"y": turn(y, d)})

    def second(zr):
        for d in range(3):
            glanded(kf.at[zr, x, y, :, cs], zr * 12 + d)
        for d in range(1, 4):
            gpush(kf.at[zr, :, y, :, cs], kf.at[zr, :, y, :, cs], zr * 12 + 6 + d - 1, {"y": turn(y, d)})
        for d in range(3):
            glanded(vf.at[zr, x, y, :, cs], zr * 12 + 3 + d)
        for d in range(1, 4):
            gpush(vf.at[zr, x, :, :, cs], vf.at[zr, x, :, :, cs], zr * 12 + 9 + d - 1, {"x": turn(x, d)})

    def third(zr):
        for d in range(3):
            glanded(kf.at[zr, :, y, :, cs], zr * 12 + 6 + d)
        gpush(kf.at[zr, :, :, :, cs], kf.at[zr, :, :, :, cs], 32 + zr, {"core": 1 - core})
        for d in range(3):
            glanded(vf.at[zr, x, :, :, cs], zr * 12 + 9 + d)
        gpush(vf.at[zr, :, :, :, cs], vf.at[zr, :, :, :, cs], 34 + zr, {"core": 1 - core})

    def swapped(zr):
        glanded(kf.at[zr, :, :, :, other], 32 + zr)
        glanded(vf.at[zr, :, :, :, other], 34 + zr)

    @pl.when(edge)
    def _():
        base = jnp.where(zl == 0, 4, 0)
        for t in range(4):
            to = {"zh": 1 - zh, "zl": base + t}
            push(kp.at[:, cs], kf.at[1, x, y, :, cs], gs.at[24 + t], gr.at[24], to)
            push(vp.at[:, cs], vf.at[1, x, y, :, cs], gs.at[28 + t], gr.at[25], to)

    first(0)
    for d in (4, 12):
        pl.semaphore_signal(known, 1, device_id=along_z(d), device_id_type=MESH)
    for c in loads[2:]:
        c.wait()
    headT = lax.div(eT[...], 8)
    for p in range(TOPK):
        rows = slice(p * 128, (p + 1) * 128)
        hc = jnp.transpose(jnp.broadcast_to(headT[p : p + 1, :].astype(F32), (128, 128)))
        q32 = q[:, rows].astype(F32)
        d32 = do[:, rows].astype(F32)
        for h in range(KV_HEADS):
            mine = hc == float(h)
            cols = slice(h * 128, (h + 1) * 128)
            qx[rows, cols] = jnp.where(mine, q32, 0.0).astype(BF16)
            dx[rows, cols] = jnp.where(mine, d32, 0.0).astype(BF16)
    for c in loads[:2]:
        c.wait()
    second(0)
    glanded(kf.at[1, x, y, :, cs], 24)
    glanded(vf.at[1, x, y, :, cs], 25)
    first(1)
    third(0)
    second(1)
    swapped(0)
    k0, v0 = kf[0].reshape(256, 1024), vf[0].reshape(256, 1024)
    for kk in range(8):
        rows = pl.ds(kk * 256, 256)
        s0[:, rows] = lax.dot_general(k0, qx[rows, :], NT, preferred_element_type=F32)
        d0[:, rows] = lax.dot_general(v0, dx[rows, :], NT, preferred_element_type=F32)
    third(1)
    swapped(1)

    block = ((zl * 2 + core) * 32) + ((x * 2 + zh) * 4 + y)
    per = CLEN // ROWS
    length = len_ref[lax.div(block, per)]
    token = lax.broadcasted_iota(jnp.int32, (1, ROWS), 1) + lax.rem(block, per) * ROWS
    live = (token < length).astype(F32)
    lv = jnp.concatenate([live, live], axis=1)
    k1, v1 = kf[1].reshape(256, 1024), vf[1].reshape(256, 1024)
    for kk in range(8):
        rows = pl.ds(kk * 256, 256)
        s = jnp.concatenate(
            [s0[:, rows], lax.dot_general(k1, qx[rows, :], NT, preferred_element_type=F32)], axis=0
        )
        dp = jnp.concatenate(
            [d0[:, rows], lax.dot_general(v1, dx[rows, :], NT, preferred_element_type=F32)], axis=0
        )
        m = jnp.max(s, axis=0, keepdims=True)
        e = jnp.exp2((s - m) * (SCALE * LOG2E))
        inv = 1.0 / jnp.sum(e, axis=0, keepdims=True)
        g = jnp.sum(e * dp, axis=0, keepdims=True) * inv
        gate = jnp.concatenate([gT[2 * kk : 2 * kk + 1, :], gT[2 * kk + 1 : 2 * kk + 2, :]], axis=1)
        w = e * (gate * lv * inv)
        pf[:, rows] = w.astype(BF16)
        ds[:, rows] = (w * (dp - g)).astype(BF16)
        gg = g * lv
        ggT[2 * kk : 2 * kk + 1, :] = gg[:, :128]
        ggT[2 * kk + 1 : 2 * kk + 2, :] = gg[:, 128:]

    def product(u, base, n):
        left_side, right_side = ((pf, dx), (ds, qx))[u]
        cols = pl.ds(pl.multiple_of(base * 512 + n * 256, 256), 256)
        made = lax.dot_general(left_side[...], right_side[:, cols], NN, preferred_element_type=F32)
        if u == 1:
            made = made * SCALE
        return made.reshape(2, 4, 4, 16, 256)

    def send0(u, n):
        far[u, n] = product(u, 1 - core, n).astype(BF16)
        at = u * 2 + n
        push(far.at[u, n], r0.at[u, n], ss.at[at], rs.at[at], {"core": 1 - core})

    def send1(u, n):
        near[...] = product(u, core, n)
        at = u * 2 + n
        landed(r0.at[u, n], ss.at[at], rs.at[at], me)
        p0[u, n] = (near[...] + r0[u, n].astype(F32)).astype(BF16)
        for d in range(1, 4):
            at = 4 + (u * 2 + n) * 3 + d - 1
            if n == 0:
                xp = turn(x, d)
                push(p0.at[u, n, :, xp], r1.at[u, n, d - 1], ss.at[at], rs.at[at], {"x": xp})
            else:
                yp = turn(y, d)
                push(p0.at[u, n, :, :, yp], r1.at[u, n, d - 1], ss.at[at], rs.at[at], {"y": yp})

    def send2(u):
        for n in range(2):
            for d in range(3):
                at = 4 + (u * 2 + n) * 3 + d
                landed(r1.at[u, n, d], ss.at[at], rs.at[at], me)
            own = p0[u, n, :, x] if n == 0 else p0[u, n, :, :, y]
            acc = own.astype(F32)
            for d in range(3):
                acc = acc + r1[u, n, d].astype(F32)
            p1[u, n] = acc.astype(BF16)
            for d in range(1, 4):
                at = 16 + (u * 2 + n) * 3 + d - 1
                if n == 0:
                    yp = turn(y, d)
                    push(p1.at[u, n, :, yp], r2.at[u, n, d - 1], ss.at[at], rs.at[at], {"y": yp})
                else:
                    xp = turn(x, d)
                    push(p1.at[u, n, :, xp], r2.at[u, n, d - 1], ss.at[at], rs.at[at], {"x": xp})

    def send3(u):
        for n in range(2):
            for d in range(3):
                at = 16 + (u * 2 + n) * 3 + d
                landed(r2.at[u, n, d], ss.at[at], rs.at[at], me)
            own = p1[u, n, :, y] if n == 0 else p1[u, n, :, x]
            acc = own.astype(F32)
            for d in range(3):
                acc = acc + r2[u, n, d].astype(F32)
            for j in range(2):
                p2[u, :, 2 * n + j] = acc[:, :, j * 128 : (j + 1) * 128].astype(BF16)
        for zr in range(2):
            zt = zh if zr == 0 else 1 - zh
            for j in range(4):
                at = 28 + u * 8 + zr * 4 + j

                def go(zr=zr, zt=zt, j=j, at=at):
                    push(
                        p2.at[u, zr, j], r3.at[u, zr, zl], ss.at[at], rs.at[28 + u * 16 + zr * 8 + zl],
                        {"zh": zt, "zl": 2 + j},
                    )

                if zr == 0:
                    pl.when(zl != 2 + j)(go)
                else:
                    go()

    def send4(u):
        @pl.when(owner)
        def _():
            for zr in range(2):
                for t in range(8):
                    def get(zr=zr, t=t):
                        landed(r3.at[u, zr, t], ss.at[28], rs.at[28 + u * 16 + zr * 8 + t], me)

                    if zr == 0:
                        pl.when(zl != t)(get)
                    else:
                        get()
            r3[u, 0, zl] = p2[u, 0, mine_j]
            acc = r3[u, 0, 0].astype(F32)
            for i in range(1, 16):
                acc = acc + r3[u, i // 8, i % 8].astype(F32)
            fin[u, core, mine_j] = acc.astype(BF16)
            for c in range(2):
                for t in range(8):
                    def go(c=c, t=t):
                        push(
                            fin.at[u, core, mine_j], fin.at[u, core, mine_j], ss.at[44 + u * 16 + c * 8 + t],
                            rs.at[60 + u * 8 + core * 4 + mine_j], {"core": c, "zl": t},
                        )

                    pl.when(jnp.logical_or(core != c, zl != t))(go)

    def finish(u, out):
        for c in range(2):
            for j in range(4):
                @pl.when(jnp.logical_or(core != c, zl != 2 + j))
                def _(c=c, j=j):
                    landed(fin.at[u, c, j], ss.at[44], rs.at[60 + u * 8 + c * 4 + j], me)

                out[:, (c * 4 + j) * 128 : (c * 4 + j + 1) * 128] = fin[u, c, j].astype(F32)

    def rows_out(src, mat, out, by):
        for kk in range(8):
            hd = jnp.concatenate([headT[2 * kk : 2 * kk + 1, :], headT[2 * kk + 1 : 2 * kk + 2, :]], axis=1)
            full = lax.dot_general(mat[...], src[:, kk * 256 : (kk + 1) * 256], NN, preferred_element_type=F32)
            acc = full[:128, :]
            for h in range(1, KV_HEADS):
                acc = jnp.where(hd == h, full[h * 128 : (h + 1) * 128, :], acc)
            acc = acc * by
            for j in range(2):
                at = (2 * kk + j) * 128
                out[:, at : at + 128] = jnp.transpose(acc[:, j * 128 : (j + 1) * 128]).astype(BF16)

    for u in range(2):
        send0(u, 0)
        send0(u, 1)
        send1(u, 0)
        send1(u, 1)
    send2(0)
    send2(1)
    pl.semaphore_wait(known, 2)
    pl.semaphore_signal(both, 1, device_id={"core": 1 - core}, device_id_type=MESH)
    send3(0)
    send3(1)
    vt[...] = jnp.transpose(vf[...].reshape(512, 1024))
    rows_out(pf, vt, att, 1.0)
    pl.semaphore_wait(both, 1)
    send4(0)
    kt[...] = jnp.transpose(kf[...].reshape(512, 1024))
    rows_out(ds, kt, dq, SCALE)
    send4(1)
    finish(0, out_v)
    finish(1, out_k)

    for zr in range(2):
        for d in range(3):
            left(kf.at[zr, x, y, :, cs], gs.at[zr * 12 + d], gr.at[0], me)
            left(vf.at[zr, x, y, :, cs], gs.at[zr * 12 + 3 + d], gr.at[0], me)
            left(kf.at[zr, :, y, :, cs], gs.at[zr * 12 + 6 + d], gr.at[0], me)
            left(vf.at[zr, x, :, :, cs], gs.at[zr * 12 + 9 + d], gr.at[0], me)
        left(kf.at[zr, :, :, :, cs], gs.at[32 + zr], gr.at[0], me)
        left(vf.at[zr, :, :, :, cs], gs.at[34 + zr], gr.at[0], me)

    @pl.when(edge)
    def _():
        for t in range(8):
            left(kf.at[0, x, y, :, cs], gs.at[24 + t], gr.at[0], me)

    for u in range(2):
        for n in range(2):
            left(far.at[u, n], ss.at[u * 2 + n], rs.at[0], me)
            for d in range(3):
                left(r1.at[u, n, d], ss.at[4 + (u * 2 + n) * 3 + d], rs.at[0], me)
                left(r2.at[u, n, d], ss.at[16 + (u * 2 + n) * 3 + d], rs.at[0], me)
        for zr in range(2):
            for j in range(4):
                def done(u=u, zr=zr, j=j):
                    left(p2.at[u, zr, j], ss.at[28 + u * 8 + zr * 4 + j], rs.at[0], me)

                if zr == 0:
                    pl.when(zl != 2 + j)(done)
                else:
                    done()
    @pl.when(owner)
    def _():
        for u in range(2):
            for c in range(2):
                for t in range(8):
                    @pl.when(jnp.logical_or(core != c, zl != t))
                    def _(u=u, c=c, t=t):
                        left(fin.at[0, 0, 0], ss.at[44 + u * 16 + c * 8 + t], rs.at[0], me)


def copy_kernel(*refs):
    given, made, held, sem_in, sem_out = refs[:5], refs[5:10], refs[10:15], refs[15], refs[16]
    ins = [pltpu.make_async_copy(given[i], held[i], sem_in.at[i]) for i in range(5)]
    outs = [pltpu.make_async_copy(held[i], made[i], sem_out.at[i]) for i in range(5)]
    for c in ins:
        c.start()
    for i in range(5):
        ins[i].wait()
        outs[i].start()
    for c in outs:
        c.wait()


def local(queries, experts, gate, prefix_keys, prefix_values, d_out, lengths):
    rows = jax.ShapeDtypeStruct((ROWS, TOPK * HEAD), BF16)
    owned = jax.ShapeDtypeStruct((16, 1024), F32)
    HBM = pl.BlockSpec(memory_space=pltpu.HBM)
    full = pltpu.VMEM((2, 4, 4, 16, 1024), BF16)
    att, dq, ggT, key_grad, value_grad = pl.pallas_call(
        kernel,
        out_shape=(rows, rows, jax.ShapeDtypeStruct((TOPK, ROWS), F32), owned, owned),
        in_specs=[HBM] * 7,
        out_specs=(VMEM,) * 5,
        scratch_shapes=[
            pltpu.SMEM((64,), jnp.int32),
            pltpu.VMEM((TOPK, ROWS), jnp.int32),
            pltpu.VMEM((TOPK, ROWS), F32),
            pltpu.VMEM((ROWS, 2048), BF16),
            pltpu.VMEM((ROWS, 2048), BF16),
            full,
            full,
            pltpu.VMEM((2048, 1024), BF16),
            pltpu.VMEM((2048, 1024), BF16),
            pltpu.VMEM((256, 2048), F32),
            pltpu.VMEM((256, 2048), F32),
            pltpu.VMEM((512, 2048), BF16),
            pltpu.VMEM((512, 2048), BF16),
            pltpu.VMEM((1024, 512), BF16),
            pltpu.VMEM((1024, 512), BF16),
            pltpu.VMEM((2, 2, 2, 4, 4, 16, 256), BF16),
            pltpu.VMEM((2, 4, 4, 16, 256), F32),
            pltpu.VMEM((2, 2, 2, 4, 4, 16, 256), BF16),
            pltpu.VMEM((2, 2, 2, 4, 4, 16, 256), BF16),
            pltpu.VMEM((2, 2, 3, 2, 4, 16, 256), BF16),
            pltpu.VMEM((2, 2, 2, 4, 16, 256), BF16),
            pltpu.VMEM((2, 2, 3, 2, 16, 256), BF16),
            pltpu.VMEM((2, 2, 4, 16, 128), BF16),
            pltpu.VMEM((2, 2, 8, 16, 128), BF16),
            pltpu.VMEM((2, 2, 4, 16, 128), BF16),
            pltpu.SemaphoreType.DMA((7,)),
            pltpu.SemaphoreType.DMA((36,)),
            pltpu.SemaphoreType.DMA((36,)),
            pltpu.SemaphoreType.DMA((76,)),
            pltpu.SemaphoreType.DMA((76,)),
            pltpu.SemaphoreType.REGULAR,
            pltpu.SemaphoreType.REGULAR,
        ],
        compiler_params=pltpu.CompilerParams(collective_id=0, has_side_effects=True, vmem_limit_bytes=60 << 20),
        name="prefix",
    )(lengths, experts.T, gate.T, queries, d_out, prefix_keys, prefix_values)
    made = (att, dq, ggT, key_grad, value_grad)
    att, dq, ggT, key_grad, value_grad = pl.pallas_call(
        copy_kernel,
        out_shape=tuple(jax.ShapeDtypeStruct(a.shape, a.dtype) for a in made),
        in_specs=[HBM] * 5,
        out_specs=(HBM,) * 5,
        scratch_shapes=[pltpu.VMEM(a.shape, a.dtype) for a in made] + [pltpu.SemaphoreType.DMA((5,))] * 2,
        compiler_params=pltpu.CompilerParams(vmem_limit_bytes=60 << 20),
        name="results",
    )(*made)
    return att, dq, ggT.T, key_grad, value_grad


def solution(mesh):
    torus = Mesh(mesh.devices.reshape(8, 2, 4, 2, 4), AXES)
    in_specs = (P(AXES, None), P(AXES, None), P(AXES, None), P(CTX, None), P(CTX, None), P(AXES, None), P())
    out_specs = (P(AXES, None), P(AXES, None), P(AXES, None), P(CTX, None), P(CTX, None))
    return jax.shard_map(local, mesh=torus, in_specs=in_specs, out_specs=out_specs, check_vma=False)
```

```python
import functools
import math

import jax
import jax.numpy as jnp
from jax import lax
from jax.experimental import pallas as pl
from jax.experimental.pallas import tpu as pltpu
from jax.sharding import Mesh
from jax.sharding import PartitionSpec as P

HEAD = 128
KV_HEADS = 8
TOPK = 16
CLEN = 1024
ROWS = 128
AXES = ("zl", "core", "x", "zh", "y")
CTX = ("x", "zh", "y")
NT = (((1,), (1,)), ((), ()))
NN = (((1,), (0,)), ((), ()))
SCALE = HEAD ** (-0.5)
LOG2E = math.log2(math.e)
F32 = jnp.float32
BF16 = jnp.bfloat16
MESH = pl.DeviceIdType.MESH
VMEM = pl.BlockSpec(memory_space=pltpu.VMEM)
SMEM = pl.BlockSpec(memory_space=pltpu.SMEM)


def place():
    return tuple(lax.axis_index(a) for a in AXES)


def push(src, dst, send, recv, to):
    copy = pltpu.make_async_remote_copy(
        src_ref=src, dst_ref=dst, send_sem=send, recv_sem=recv, device_id=to, device_id_type=MESH
    )
    copy.start()
    return copy


def landed(ref, send, recv, me):
    pltpu.make_async_remote_copy(
        src_ref=ref, dst_ref=ref, send_sem=send, recv_sem=recv, device_id=me, device_id_type=MESH
    ).wait_recv()


def left(ref, send, recv, me):
    pltpu.make_async_remote_copy(
        src_ref=ref, dst_ref=ref, send_sem=send, recv_sem=recv, device_id=me, device_id_type=MESH
    ).wait_send()


def turn(i, d):
    return lax.rem(i + d, 4)


def half(core):
    return pl.ds(pl.multiple_of(core * 512, 512), 512)


def kernel(
    len_in, eT_in, gT_in, q_in, d_in, kp, vp,
    att, dq, ggT, out_k, out_v,
    len_ref, eT, gT, q, do, kf, vf, qx, dx, s0, d0, pf, ds, vt, kt,
    far, near, r0, p0, r1, p1, r2, p2, r3, fin, ls, gs, gr, ss, rs, known, both,
):
    zl, core, x, zh, y = place()
    me = (zl, core, x, zh, y)
    cs, other = half(core), half(1 - core)
    owner, mine_j = jnp.logical_and(zl >= 2, zl < 6), jnp.clip(zl - 2, 0, 3)
    edge = jnp.logical_or(zl == 0, zl == 7)

    loads = [
        pltpu.make_async_copy(kp.at[:, cs], kf.at[0, x, y, :, cs], ls.at[0]),
        pltpu.make_async_copy(vp.at[:, cs], vf.at[0, x, y, :, cs], ls.at[1]),
        pltpu.make_async_copy(eT_in, eT, ls.at[2]),
        pltpu.make_async_copy(gT_in, gT, ls.at[3]),
        pltpu.make_async_copy(q_in, q, ls.at[4]),
        pltpu.make_async_copy(d_in, do, ls.at[5]),
        pltpu.make_async_copy(len_in, len_ref, ls.at[6]),
    ]
    for c in loads:
        c.start()

    def along_z(d):
        z = lax.rem(zh * 8 + zl + d, 16)
        return {"zh": lax.div(z, 8), "zl": lax.rem(z, 8)}

    barrier = pltpu.get_barrier_semaphore()
    for d in range(1, 4):
        pl.semaphore_signal(barrier, 1, device_id={"x": turn(x, d)}, device_id_type=MESH)
        pl.semaphore_signal(barrier, 1, device_id={"y": turn(y, d)}, device_id_type=MESH)
    pl.semaphore_signal(barrier, 1, device_id={"core": 1 - core}, device_id_type=MESH)
    for d in (1, 2, 3, 4, 12, 13, 14, 15):
        pl.semaphore_signal(barrier, 1, device_id=along_z(d), device_id_type=MESH)
    pl.semaphore_wait(barrier, 15)

    def gpush(src, dst, at, to):
        push(src, dst, gs.at[at], gr.at[at], to)

    def glanded(ref, at):
        landed(ref, gs.at[at], gr.at[at], me)

    whole, given = (kf, vf), (kp, vp)
    ca = pl.ds(pl.multiple_of(core * 512, 256), 256)
    cb = pl.ds(pl.multiple_of(core * 512 + 256, 256), 256)

    def first(m, zr):
        at, ref = (m * 2 + zr) * 13, whole[m]
        for d in range(1, 4):
            for n, cols, to in ((0, ca, {"x": turn(x, d)}), (3, cb, {"y": turn(y, d)})):
                src = given[m].at[:, cols] if zr == 0 else ref.at[1, x, y, :, cols]
                gpush(src, ref.at[zr, x, y, :, cols], at + n + d - 1, to)

    def second(m, zr):
        at, ref = (m * 2 + zr) * 13, whole[m]
        for d in range(3):
            glanded(ref.at[zr, x, y, :, ca], at + d)
        for d in range(1, 4):
            gpush(ref.at[zr, :, y, :, ca], ref.at[zr, :, y, :, ca], at + 6 + d - 1, {"y": turn(y, d)})
        for d in range(3):
            glanded(ref.at[zr, x, y, :, cb], at + 3 + d)
        for d in range(1, 4):
            gpush(ref.at[zr, x, :, :, cb], ref.at[zr, x, :, :, cb], at + 9 + d - 1, {"x": turn(x, d)})

    def third(m, zr):
        at, ref = (m * 2 + zr) * 13, whole[m]
        for d in range(3):
            glanded(ref.at[zr, :, y, :, ca], at + 6 + d)
            glanded(ref.at[zr, x, :, :, cb], at + 9 + d)
        gpush(ref.at[zr, :, :, :, cs], ref.at[zr, :, :, :, cs], at + 12, {"core": 1 - core})

    def swapped(m, zr):
        glanded(whole[m].at[zr, :, :, :, other], (m * 2 + zr) * 13 + 12)

    def across(m):
        @pl.when(edge)
        def _():
            base = jnp.where(zl == 0, 4, 0)
            for t in range(4):
                to = {"zh": 1 - zh, "zl": base + t}
                push(given[m].at[:, cs], whole[m].at[1, x, y, :, cs], gs.at[54 + m * 4 + t], gr.at[52 + m], to)

    def crossed(m):
        glanded(whole[m].at[1, x, y, :, cs], 52 + m)

    across(0)
    first(0, 0)
    for d in (4, 12):
        pl.semaphore_signal(known, 1, device_id=along_z(d), device_id_type=MESH)
    for c in loads[2:]:
        c.wait()
    headT = lax.div(eT[...], 8)
    for p in range(TOPK):
        rows = slice(p * 128, (p + 1) * 128)
        hc = jnp.transpose(jnp.broadcast_to(headT[p : p + 1, :].astype(F32), (128, 128)))
        q32 = q[:, rows].astype(F32)
        d32 = do[:, rows].astype(F32)
        for h in range(KV_HEADS):
            mine = hc == float(h)
            cols = slice(h * 128, (h + 1) * 128)
            qx[rows, cols] = jnp.where(mine, q32, 0.0).astype(BF16)
            dx[rows, cols] = jnp.where(mine, d32, 0.0).astype(BF16)
    for c in loads[:2]:
        c.wait()
    second(0, 0)
    across(1)
    first(1, 0)
    crossed(0)
    first(0, 1)
    third(0, 0)
    second(1, 0)
    second(0, 1)
    crossed(1)
    first(1, 1)
    swapped(0, 0)
    k0 = kf[0].reshape(256, 1024)
    for kk in range(8):
        rows = pl.ds(kk * 256, 256)
        s0[:, rows] = lax.dot_general(k0, qx[rows, :], NT, preferred_element_type=F32)
    third(1, 0)
    third(0, 1)
    second(1, 1)
    swapped(1, 0)
    v0 = vf[0].reshape(256, 1024)
    for kk in range(8):
        rows = pl.ds(kk * 256, 256)
        d0[:, rows] = lax.dot_general(v0, dx[rows, :], NT, preferred_element_type=F32)
    swapped(0, 1)

    block = ((zl * 2 + core) * 32) + ((x * 2 + zh) * 4 + y)
    per = CLEN // ROWS
    length = len_ref[lax.div(block, per)]
    token = lax.broadcasted_iota(jnp.int32, (1, ROWS), 1) + lax.rem(block, per) * ROWS
    live = (token < length).astype(F32)
    lv = jnp.concatenate([live, live], axis=1)
    k1 = kf[1].reshape(256, 1024)

    def gates(kk):
        return jnp.concatenate([gT[2 * kk : 2 * kk + 1, :], gT[2 * kk + 1 : 2 * kk + 2, :]], axis=1)

    for kk in range(8):
        rows = pl.ds(kk * 256, 256)
        s = jnp.concatenate(
            [s0[:, rows], lax.dot_general(k1, qx[rows, :], NT, preferred_element_type=F32)], axis=0
        )
        m = jnp.max(s, axis=0, keepdims=True)
        e = jnp.exp2((s - m) * (SCALE * LOG2E))
        inv = 1.0 / jnp.sum(e, axis=0, keepdims=True)
        pf[:, rows] = (e * (gates(kk) * lv * inv)).astype(BF16)

    def product(u, base, n):
        left_side, right_side = ((pf, dx), (ds, qx))[u]
        cols = pl.ds(pl.multiple_of(base * 512 + n * 256, 256), 256)
        made = lax.dot_general(left_side[...], right_side[:, cols], NN, preferred_element_type=F32)
        if u == 1:
            made = made * SCALE
        return made.reshape(2, 4, 4, 16, 256)

    def send0(u, n):
        far[u, n] = product(u, 1 - core, n).astype(BF16)
        at = u * 2 + n
        push(far.at[u, n], r0.at[u, n], ss.at[at], rs.at[at], {"core": 1 - core})

    def send1(u, n):
        near[...] = product(u, core, n)
        at = u * 2 + n
        landed(r0.at[u, n], ss.at[at], rs.at[at], me)
        p0[u, n] = (near[...] + r0[u, n].astype(F32)).astype(BF16)
        for d in range(1, 4):
            at = 4 + (u * 2 + n) * 3 + d - 1
            if n == 0:
                xp = turn(x, d)
                push(p0.at[u, n, :, xp], r1.at[u, n, d - 1], ss.at[at], rs.at[at], {"x": xp})
            else:
                yp = turn(y, d)
                push(p0.at[u, n, :, :, yp], r1.at[u, n, d - 1], ss.at[at], rs.at[at], {"y": yp})

    def send2(u):
        for n in range(2):
            for d in range(3):
                at = 4 + (u * 2 + n) * 3 + d
                landed(r1.at[u, n, d], ss.at[at], rs.at[at], me)
            own = p0[u, n, :, x] if n == 0 else p0[u, n, :, :, y]
            acc = own.astype(F32)
            for d in range(3):
                acc = acc + r1[u, n, d].astype(F32)
            p1[u, n] = acc.astype(BF16)
            for d in range(1, 4):
                at = 16 + (u * 2 + n) * 3 + d - 1
                if n == 0:
                    yp = turn(y, d)
                    push(p1.at[u, n, :, yp], r2.at[u, n, d - 1], ss.at[at], rs.at[at], {"y": yp})
                else:
                    xp = turn(x, d)
                    push(p1.at[u, n, :, xp], r2.at[u, n, d - 1], ss.at[at], rs.at[at], {"x": xp})

    def send3(u):
        for n in range(2):
            for d in range(3):
                at = 16 + (u * 2 + n) * 3 + d
                landed(r2.at[u, n, d], ss.at[at], rs.at[at], me)
            own = p1[u, n, :, y] if n == 0 else p1[u, n, :, x]
            acc = own.astype(F32)
            for d in range(3):
                acc = acc + r2[u, n, d].astype(F32)
            for j in range(2):
                p2[u, :, 2 * n + j] = acc[:, :, j * 128 : (j + 1) * 128].astype(BF16)
        for zr in range(2):
            zt = zh if zr == 0 else 1 - zh
            for j in range(4):
                at = 28 + u * 8 + zr * 4 + j

                def go(zr=zr, zt=zt, j=j, at=at):
                    push(
                        p2.at[u, zr, j], r3.at[u, zr, zl], ss.at[at], rs.at[28 + u * 16 + zr * 8 + zl],
                        {"zh": zt, "zl": 2 + j},
                    )

                if zr == 0:
                    pl.when(zl != 2 + j)(go)
                else:
                    go()

    def send4(u):
        @pl.when(owner)
        def _():
            for zr in range(2):
                for t in range(8):
                    def get(zr=zr, t=t):
                        landed(r3.at[u, zr, t], ss.at[28], rs.at[28 + u * 16 + zr * 8 + t], me)

                    if zr == 0:
                        pl.when(zl != t)(get)
                    else:
                        get()
            r3[u, 0, zl] = p2[u, 0, mine_j]
            acc = r3[u, 0, 0].astype(F32)
            for i in range(1, 16):
                acc = acc + r3[u, i // 8, i % 8].astype(F32)
            fin[u, core, mine_j] = acc.astype(BF16)
            for c in range(2):
                for t in range(8):
                    def go(c=c, t=t):
                        push(
                            fin.at[u, core, mine_j], fin.at[u, core, mine_j], ss.at[44 + u * 16 + c * 8 + t],
                            rs.at[60 + u * 8 + core * 4 + mine_j], {"core": c, "zl": t},
                        )

                    pl.when(jnp.logical_or(core != c, zl != t))(go)

    def finish(u, out):
        for c in range(2):
            for j in range(4):
                @pl.when(jnp.logical_or(core != c, zl != 2 + j))
                def _(c=c, j=j):
                    landed(fin.at[u, c, j], ss.at[44], rs.at[60 + u * 8 + c * 4 + j], me)

                out[:, (c * 4 + j) * 128 : (c * 4 + j + 1) * 128] = fin[u, c, j].astype(F32)

    def rows_out(src, mat, out, by):
        for kk in range(8):
            hd = jnp.concatenate([headT[2 * kk : 2 * kk + 1, :], headT[2 * kk + 1 : 2 * kk + 2, :]], axis=1)
            full = lax.dot_general(mat[...], src[:, kk * 256 : (kk + 1) * 256], NN, preferred_element_type=F32)
            acc = full[:128, :]
            for h in range(1, KV_HEADS):
                acc = jnp.where(hd == h, full[h * 128 : (h + 1) * 128, :], acc)
            acc = acc * by
            for j in range(2):
                at = (2 * kk + j) * 128
                out[:, at : at + 128] = jnp.transpose(acc[:, j * 128 : (j + 1) * 128]).astype(BF16)

    third(1, 1)
    send0(0, 0)
    send0(0, 1)
    send1(0, 0)
    send1(0, 1)
    swapped(1, 1)
    v1 = vf[1].reshape(256, 1024)
    for kk in range(8):
        rows = pl.ds(kk * 256, 256)
        dp = jnp.concatenate(
            [d0[:, rows], lax.dot_general(v1, dx[rows, :], NT, preferred_element_type=F32)], axis=0
        )
        w = pf[:, rows].astype(F32)
        g = jnp.sum(w * dp, axis=0, keepdims=True) / gates(kk)
        ds[:, rows] = (w * (dp - g)).astype(BF16)
        ggT[2 * kk : 2 * kk + 1, :] = g[:, :128]
        ggT[2 * kk + 1 : 2 * kk + 2, :] = g[:, 128:]
    send0(1, 0)
    send0(1, 1)
    send1(1, 0)
    send1(1, 1)
    send2(0)
    send2(1)
    pl.semaphore_wait(known, 2)
    pl.semaphore_signal(both, 1, device_id={"core": 1 - core}, device_id_type=MESH)
    send3(0)
    send3(1)
    vt[...] = jnp.transpose(vf[...].reshape(512, 1024))
    rows_out(pf, vt, att, 1.0)
    pl.semaphore_wait(both, 1)
    send4(0)
    kt[...] = jnp.transpose(kf[...].reshape(512, 1024))
    rows_out(ds, kt, dq, SCALE)
    send4(1)
    finish(0, out_v)
    finish(1, out_k)

    for m in range(2):
        for zr in range(2):
            at, ref = (m * 2 + zr) * 13, whole[m]
            for d in range(3):
                left(ref.at[zr, x, y, :, ca], gs.at[at + d], gr.at[0], me)
                left(ref.at[zr, x, y, :, cb], gs.at[at + 3 + d], gr.at[0], me)
                left(ref.at[zr, :, y, :, ca], gs.at[at + 6 + d], gr.at[0], me)
                left(ref.at[zr, x, :, :, cb], gs.at[at + 9 + d], gr.at[0], me)
            left(ref.at[zr, :, :, :, cs], gs.at[at + 12], gr.at[0], me)

    @pl.when(edge)
    def _():
        for t in range(8):
            left(kf.at[0, x, y, :, cs], gs.at[54 + t], gr.at[0], me)

    for u in range(2):
        for n in range(2):
            left(far.at[u, n], ss.at[u * 2 + n], rs.at[0], me)
            for d in range(3):
                left(r1.at[u, n, d], ss.at[4 + (u * 2 + n) * 3 + d], rs.at[0], me)
                left(r2.at[u, n, d], ss.at[16 + (u * 2 + n) * 3 + d], rs.at[0], me)
        for zr in range(2):
            for j in range(4):
                def done(u=u, zr=zr, j=j):
                    left(p2.at[u, zr, j], ss.at[28 + u * 8 + zr * 4 + j], rs.at[0], me)

                if zr == 0:
                    pl.when(zl != 2 + j)(done)
                else:
                    done()
    @pl.when(owner)
    def _():
        for u in range(2):
            for c in range(2):
                for t in range(8):
                    @pl.when(jnp.logical_or(core != c, zl != t))
                    def _(u=u, c=c, t=t):
                        left(fin.at[0, 0, 0], ss.at[44 + u * 16 + c * 8 + t], rs.at[0], me)


def copy_kernel(*refs):
    given, made, held, sem_in, sem_out = refs[:5], refs[5:10], refs[10:15], refs[15], refs[16]
    ins = [pltpu.make_async_copy(given[i], held[i], sem_in.at[i]) for i in range(5)]
    outs = [pltpu.make_async_copy(held[i], made[i], sem_out.at[i]) for i in range(5)]
    for c in ins:
        c.start()
    for i in range(5):
        ins[i].wait()
        outs[i].start()
    for c in outs:
        c.wait()


def local(queries, experts, gate, prefix_keys, prefix_values, d_out, lengths):
    rows = jax.ShapeDtypeStruct((ROWS, TOPK * HEAD), BF16)
    owned = jax.ShapeDtypeStruct((16, 1024), F32)
    HBM = pl.BlockSpec(memory_space=pltpu.HBM)
    full = pltpu.VMEM((2, 4, 4, 16, 1024), BF16)
    att, dq, ggT, key_grad, value_grad = pl.pallas_call(
        kernel,
        out_shape=(rows, rows, jax.ShapeDtypeStruct((TOPK, ROWS), F32), owned, owned),
        in_specs=[HBM] * 7,
        out_specs=(VMEM,) * 5,
        scratch_shapes=[
            pltpu.SMEM((64,), jnp.int32),
            pltpu.VMEM((TOPK, ROWS), jnp.int32),
            pltpu.VMEM((TOPK, ROWS), F32),
            pltpu.VMEM((ROWS, 2048), BF16),
            pltpu.VMEM((ROWS, 2048), BF16),
            full,
            full,
            pltpu.VMEM((2048, 1024), BF16),
            pltpu.VMEM((2048, 1024), BF16),
            pltpu.VMEM((256, 2048), F32),
            pltpu.VMEM((256, 2048), F32),
            pltpu.VMEM((512, 2048), BF16),
            pltpu.VMEM((512, 2048), BF16),
            pltpu.VMEM((1024, 512), BF16),
            pltpu.VMEM((1024, 512), BF16),
            pltpu.VMEM((2, 2, 2, 4, 4, 16, 256), BF16),
            pltpu.VMEM((2, 4, 4, 16, 256), F32),
            pltpu.VMEM((2, 2, 2, 4, 4, 16, 256), BF16),
            pltpu.VMEM((2, 2, 2, 4, 4, 16, 256), BF16),
            pltpu.VMEM((2, 2, 3, 2, 4, 16, 256), BF16),
            pltpu.VMEM((2, 2, 2, 4, 16, 256), BF16),
            pltpu.VMEM((2, 2, 3, 2, 16, 256), BF16),
            pltpu.VMEM((2, 2, 4, 16, 128), BF16),
            pltpu.VMEM((2, 2, 8, 16, 128), BF16),
            pltpu.VMEM((2, 2, 4, 16, 128), BF16),
            pltpu.SemaphoreType.DMA((7,)),
            pltpu.SemaphoreType.DMA((62,)),
            pltpu.SemaphoreType.DMA((62,)),
            pltpu.SemaphoreType.DMA((76,)),
            pltpu.SemaphoreType.DMA((76,)),
            pltpu.SemaphoreType.REGULAR,
            pltpu.SemaphoreType.REGULAR,
        ],
        compiler_params=pltpu.CompilerParams(collective_id=0, has_side_effects=True, vmem_limit_bytes=60 << 20),
        name="prefix",
    )(lengths, experts.T, gate.T, queries, d_out, prefix_keys, prefix_values)
    made = (att, dq, ggT, key_grad, value_grad)
    att, dq, ggT, key_grad, value_grad = pl.pallas_call(
        copy_kernel,
        out_shape=tuple(jax.ShapeDtypeStruct(a.shape, a.dtype) for a in made),
        in_specs=[HBM] * 5,
        out_specs=(HBM,) * 5,
        scratch_shapes=[pltpu.VMEM(a.shape, a.dtype) for a in made] + [pltpu.SemaphoreType.DMA((5,))] * 2,
        compiler_params=pltpu.CompilerParams(vmem_limit_bytes=60 << 20),
        name="results",
    )(*made)
    return att, dq, ggT.T, key_grad, value_grad


def solution(mesh):
    torus = Mesh(mesh.devices.reshape(8, 2, 4, 2, 4), AXES)
    in_specs = (P(AXES, None), P(AXES, None), P(AXES, None), P(CTX, None), P(CTX, None), P(AXES, None), P())
    out_specs = (P(AXES, None), P(AXES, None), P(AXES, None), P(CTX, None), P(CTX, None))
    return jax.shard_map(local, mesh=torus, in_specs=in_specs, out_specs=out_specs, check_vma=False)
```

```python
import functools
import math

import jax
import jax.numpy as jnp
from jax import lax
from jax.experimental import pallas as pl
from jax.experimental.pallas import tpu as pltpu
from jax.sharding import Mesh
from jax.sharding import PartitionSpec as P

HEAD = 128
KV_HEADS = 8
TOPK = 16
CLEN = 1024
ROWS = 128
AXES = ("zl", "core", "x", "zh", "y")
CTX = ("x", "zh", "y")
NT = (((1,), (1,)), ((), ()))
NN = (((1,), (0,)), ((), ()))
SCALE = HEAD ** (-0.5)
LOG2E = math.log2(math.e)
F32 = jnp.float32
BF16 = jnp.bfloat16
MESH = pl.DeviceIdType.MESH
VMEM = pl.BlockSpec(memory_space=pltpu.VMEM)
SMEM = pl.BlockSpec(memory_space=pltpu.SMEM)


def place():
    return tuple(lax.axis_index(a) for a in AXES)


def push(src, dst, send, recv, to):
    copy = pltpu.make_async_remote_copy(
        src_ref=src, dst_ref=dst, send_sem=send, recv_sem=recv, device_id=to, device_id_type=MESH
    )
    copy.start()
    return copy


def landed(ref, send, recv, me):
    pltpu.make_async_remote_copy(
        src_ref=ref, dst_ref=ref, send_sem=send, recv_sem=recv, device_id=me, device_id_type=MESH
    ).wait_recv()


def left(ref, send, recv, me):
    pltpu.make_async_remote_copy(
        src_ref=ref, dst_ref=ref, send_sem=send, recv_sem=recv, device_id=me, device_id_type=MESH
    ).wait_send()


def turn(i, d):
    return lax.rem(i + d, 4)


def half(core):
    return pl.ds(pl.multiple_of(core * 512, 512), 512)


def kernel(
    len_in, eT_in, gT_in, q_in, d_in, kp, vp,
    att, dq, ggT, out_k, out_v,
    len_ref, eT, gT, q, do, kf, vf, qx, dx, s0, d0, pf, ds, vt, kt,
    far, near, r0, p0, r1, p1, r2, p2, r3, fin, ls, gs, gr, ss, rs, known, both,
):
    zl, core, x, zh, y = place()
    me = (zl, core, x, zh, y)
    cs, other = half(core), half(1 - core)
    owner, mine_j = jnp.logical_and(zl >= 2, zl < 6), jnp.clip(zl - 2, 0, 3)
    edge = jnp.logical_or(zl == 0, zl == 7)

    loads = [
        pltpu.make_async_copy(kp.at[:, cs], kf.at[0, x, y, :, cs], ls.at[0]),
        pltpu.make_async_copy(vp.at[:, cs], vf.at[0, x, y, :, cs], ls.at[1]),
        pltpu.make_async_copy(eT_in, eT, ls.at[2]),
        pltpu.make_async_copy(gT_in, gT, ls.at[3]),
        pltpu.make_async_copy(q_in, q, ls.at[4]),
        pltpu.make_async_copy(d_in, do, ls.at[5]),
        pltpu.make_async_copy(len_in, len_ref, ls.at[6]),
    ]
    for c in loads:
        c.start()

    def along_z(d):
        z = lax.rem(zh * 8 + zl + d, 16)
        return {"zh": lax.div(z, 8), "zl": lax.rem(z, 8)}

    barrier = pltpu.get_barrier_semaphore()
    for d in (2, 1, 3):
        pl.semaphore_signal(barrier, 1, device_id={"x": turn(x, d)}, device_id_type=MESH)
        pl.semaphore_signal(barrier, 1, device_id={"y": turn(y, d)}, device_id_type=MESH)
    pl.semaphore_signal(barrier, 1, device_id={"core": 1 - core}, device_id_type=MESH)
    for d in (4, 12, 3, 13, 2, 14, 1, 15):
        pl.semaphore_signal(barrier, 1, device_id=along_z(d), device_id_type=MESH)
    pl.semaphore_wait(barrier, 15)

    def gpush(src, dst, at, to):
        push(src, dst, gs.at[at], gr.at[at], to)

    def glanded(ref, at):
        landed(ref, gs.at[at], gr.at[at], me)

    def first(zr):
        for d in (2, 1, 3):
            a, b = zr * 12 + d - 1, zr * 12 + 3 + d - 1
            gpush(kp.at[:, cs] if zr == 0 else kf.at[1, x, y, :, cs], kf.at[zr, x, y, :, cs], a, {"x": turn(x, d)})
            gpush(vp.at[:, cs] if zr == 0 else vf.at[1, x, y, :, cs], vf.at[zr, x, y, :, cs], b, {"y": turn(y, d)})

    def second(zr):
        for d in range(3):
            glanded(kf.at[zr, x, y, :, cs], zr * 12 + d)
        for d in (2, 1, 3):
            gpush(kf.at[zr, :, y, :, cs], kf.at[zr, :, y, :, cs], zr * 12 + 6 + d - 1, {"y": turn(y, d)})
        for d in range(3):
            glanded(vf.at[zr, x, y, :, cs], zr * 12 + 3 + d)
        for d in (2, 1, 3):
            gpush(vf.at[zr, x, :, :, cs], vf.at[zr, x, :, :, cs], zr * 12 + 9 + d - 1, {"x": turn(x, d)})

    def third(zr):
        for d in range(3):
            glanded(kf.at[zr, :, y, :, cs], zr * 12 + 6 + d)
        gpush(kf.at[zr, :, :, :, cs], kf.at[zr, :, :, :, cs], 32 + zr, {"core": 1 - core})
        for d in range(3):
            glanded(vf.at[zr, x, :, :, cs], zr * 12 + 9 + d)
        gpush(vf.at[zr, :, :, :, cs], vf.at[zr, :, :, :, cs], 34 + zr, {"core": 1 - core})

    def swapped(zr):
        glanded(kf.at[zr, :, :, :, other], 32 + zr)
        glanded(vf.at[zr, :, :, :, other], 34 + zr)

    @pl.when(edge)
    def _():
        for t in range(4):
            to = {"zh": 1 - zh, "zl": jnp.where(zl == 0, 4 + t, 3 - t)}
            push(kp.at[:, cs], kf.at[1, x, y, :, cs], gs.at[24 + t], gr.at[24], to)
            push(vp.at[:, cs], vf.at[1, x, y, :, cs], gs.at[28 + t], gr.at[25], to)

    first(0)
    for d in (4, 12):
        pl.semaphore_signal(known, 1, device_id=along_z(d), device_id_type=MESH)
    for c in loads[2:]:
        c.wait()
    headT = lax.div(eT[...], 8)
    for p in range(TOPK):
        rows = slice(p * 128, (p + 1) * 128)
        hc = jnp.transpose(jnp.broadcast_to(headT[p : p + 1, :].astype(F32), (128, 128)))
        q32 = q[:, rows].astype(F32)
        d32 = do[:, rows].astype(F32)
        for h in range(KV_HEADS):
            mine = hc == float(h)
            cols = slice(h * 128, (h + 1) * 128)
            qx[rows, cols] = jnp.where(mine, q32, 0.0).astype(BF16)
            dx[rows, cols] = jnp.where(mine, d32, 0.0).astype(BF16)
    for c in loads[:2]:
        c.wait()
    second(0)
    glanded(kf.at[1, x, y, :, cs], 24)
    glanded(vf.at[1, x, y, :, cs], 25)
    first(1)
    third(0)
    second(1)
    swapped(0)
    k0, v0 = kf[0].reshape(256, 1024), vf[0].reshape(256, 1024)
    for kk in range(8):
        rows = pl.ds(kk * 256, 256)
        s0[:, rows] = lax.dot_general(k0, qx[rows, :], NT, preferred_element_type=F32)
        d0[:, rows] = lax.dot_general(v0, dx[rows, :], NT, preferred_element_type=F32)
    third(1)
    swapped(1)

    block = ((zl * 2 + core) * 32) + ((x * 2 + zh) * 4 + y)
    per = CLEN // ROWS
    length = len_ref[lax.div(block, per)]
    token = lax.broadcasted_iota(jnp.int32, (1, ROWS), 1) + lax.rem(block, per) * ROWS
    live = (token < length).astype(F32)
    lv = jnp.concatenate([live, live], axis=1)
    k1, v1 = kf[1].reshape(256, 1024), vf[1].reshape(256, 1024)
    for kk in range(8):
        rows = pl.ds(kk * 256, 256)
        s = jnp.concatenate(
            [s0[:, rows], lax.dot_general(k1, qx[rows, :], NT, preferred_element_type=F32)], axis=0
        )
        dp = jnp.concatenate(
            [d0[:, rows], lax.dot_general(v1, dx[rows, :], NT, preferred_element_type=F32)], axis=0
        )
        m = jnp.max(s, axis=0, keepdims=True)
        e = jnp.exp2((s - m) * (SCALE * LOG2E))
        inv = 1.0 / jnp.sum(e, axis=0, keepdims=True)
        g = jnp.sum(e * dp, axis=0, keepdims=True) * inv
        gate = jnp.concatenate([gT[2 * kk : 2 * kk + 1, :], gT[2 * kk + 1 : 2 * kk + 2, :]], axis=1)
        w = e * (gate * lv * inv)
        pf[:, rows] = w.astype(BF16)
        ds[:, rows] = (w * (dp - g)).astype(BF16)
        gg = g * lv
        ggT[2 * kk : 2 * kk + 1, :] = gg[:, :128]
        ggT[2 * kk + 1 : 2 * kk + 2, :] = gg[:, 128:]

    def product(u, base, n):
        left_side, right_side = ((pf, dx), (ds, qx))[u]
        cols = pl.ds(pl.multiple_of(base * 512 + n * 256, 256), 256)
        made = lax.dot_general(left_side[...], right_side[:, cols], NN, preferred_element_type=F32)
        if u == 1:
            made = made * SCALE
        return made.reshape(2, 4, 4, 16, 256)

    def send0(u, n):
        far[u, n] = product(u, 1 - core, n).astype(BF16)
        at = u * 2 + n
        push(far.at[u, n], r0.at[u, n], ss.at[at], rs.at[at], {"core": 1 - core})

    def send1(u, n):
        near[...] = product(u, core, n)
        at = u * 2 + n
        landed(r0.at[u, n], ss.at[at], rs.at[at], me)
        p0[u, n] = (near[...] + r0[u, n].astype(F32)).astype(BF16)
        for d in (2, 1, 3):
            at = 4 + (u * 2 + n) * 3 + d - 1
            if n == 0:
                xp = turn(x, d)
                push(p0.at[u, n, :, xp], r1.at[u, n, d - 1], ss.at[at], rs.at[at], {"x": xp})
            else:
                yp = turn(y, d)
                push(p0.at[u, n, :, :, yp], r1.at[u, n, d - 1], ss.at[at], rs.at[at], {"y": yp})

    def send2(u):
        for n in range(2):
            for d in range(3):
                at = 4 + (u * 2 + n) * 3 + d
                landed(r1.at[u, n, d], ss.at[at], rs.at[at], me)
            own = p0[u, n, :, x] if n == 0 else p0[u, n, :, :, y]
            acc = own.astype(F32)
            for d in range(3):
                acc = acc + r1[u, n, d].astype(F32)
            p1[u, n] = acc.astype(BF16)
            for d in (2, 1, 3):
                at = 16 + (u * 2 + n) * 3 + d - 1
                if n == 0:
                    yp = turn(y, d)
                    push(p1.at[u, n, :, yp], r2.at[u, n, d - 1], ss.at[at], rs.at[at], {"y": yp})
                else:
                    xp = turn(x, d)
                    push(p1.at[u, n, :, xp], r2.at[u, n, d - 1], ss.at[at], rs.at[at], {"x": xp})

    def send3(u):
        for n in range(2):
            for d in range(3):
                at = 16 + (u * 2 + n) * 3 + d
                landed(r2.at[u, n, d], ss.at[at], rs.at[at], me)
            own = p1[u, n, :, y] if n == 0 else p1[u, n, :, x]
            acc = own.astype(F32)
            for d in range(3):
                acc = acc + r2[u, n, d].astype(F32)
            for j in range(2):
                p2[u, :, 2 * n + j] = acc[:, :, j * 128 : (j + 1) * 128].astype(BF16)
        for zr in (1, 0):
            zt = zh if zr == 0 else 1 - zh
            for j in range(4):
                at = 28 + u * 8 + zr * 4 + j

                def go(zr=zr, zt=zt, j=j, at=at):
                    push(
                        p2.at[u, zr, j], r3.at[u, zr, zl], ss.at[at], rs.at[28 + u * 16 + zr * 8 + zl],
                        {"zh": zt, "zl": 2 + j},
                    )

                if zr == 0:
                    pl.when(zl != 2 + j)(go)
                else:
                    go()

    def send4(u):
        @pl.when(owner)
        def _():
            for zr in range(2):
                for t in range(8):
                    def get(zr=zr, t=t):
                        landed(r3.at[u, zr, t], ss.at[28], rs.at[28 + u * 16 + zr * 8 + t], me)

                    if zr == 0:
                        pl.when(zl != t)(get)
                    else:
                        get()
            r3[u, 0, zl] = p2[u, 0, mine_j]
            acc = r3[u, 0, 0].astype(F32)
            for i in range(1, 16):
                acc = acc + r3[u, i // 8, i % 8].astype(F32)
            fin[u, core, mine_j] = acc.astype(BF16)
            for t in (7, 0, 6, 1, 5, 2, 4, 3):
                for c in range(2):
                    def go(c=c, t=t):
                        push(
                            fin.at[u, core, mine_j], fin.at[u, core, mine_j], ss.at[44 + u * 16 + c * 8 + t],
                            rs.at[60 + u * 8 + core * 4 + mine_j], {"core": c, "zl": t},
                        )

                    pl.when(jnp.logical_or(core != c, zl != t))(go)

    def finish(u, out):
        for c in range(2):
            for j in range(4):
                @pl.when(jnp.logical_or(core != c, zl != 2 + j))
                def _(c=c, j=j):
                    landed(fin.at[u, c, j], ss.at[44], rs.at[60 + u * 8 + c * 4 + j], me)

                out[:, (c * 4 + j) * 128 : (c * 4 + j + 1) * 128] = fin[u, c, j].astype(F32)

    def rows_out(src, mat, out, by):
        for kk in range(8):
            hd = jnp.concatenate([headT[2 * kk : 2 * kk + 1, :], headT[2 * kk + 1 : 2 * kk + 2, :]], axis=1)
            full = lax.dot_general(mat[...], src[:, kk * 256 : (kk + 1) * 256], NN, preferred_element_type=F32)
            acc = full[:128, :]
            for h in range(1, KV_HEADS):
                acc = jnp.where(hd == h, full[h * 128 : (h + 1) * 128, :], acc)
            acc = acc * by
            for j in range(2):
                at = (2 * kk + j) * 128
                out[:, at : at + 128] = jnp.transpose(acc[:, j * 128 : (j + 1) * 128]).astype(BF16)

    send0(0, 0)
    send0(0, 1)
    send0(1, 0)
    send1(0, 0)
    send1(0, 1)
    send0(1, 1)
    send1(1, 0)
    send1(1, 1)
    send2(0)
    send2(1)
    pl.semaphore_wait(known, 2)
    pl.semaphore_signal(both, 1, device_id={"core": 1 - core}, device_id_type=MESH)
    send3(0)
    send3(1)
    vt[...] = jnp.transpose(vf[...].reshape(512, 1024))
    rows_out(pf, vt, q, 1.0)
    att_out = pltpu.make_async_copy(q, att, ls.at[0])
    att_out.start()
    for zr in range(2):
        for d in range(3):
            left(kf.at[zr, x, y, :, cs], gs.at[zr * 12 + d], gr.at[0], me)
            left(vf.at[zr, x, y, :, cs], gs.at[zr * 12 + 3 + d], gr.at[0], me)
            left(kf.at[zr, :, y, :, cs], gs.at[zr * 12 + 6 + d], gr.at[0], me)
            left(vf.at[zr, x, :, :, cs], gs.at[zr * 12 + 9 + d], gr.at[0], me)
        left(kf.at[zr, :, :, :, cs], gs.at[32 + zr], gr.at[0], me)
        left(vf.at[zr, :, :, :, cs], gs.at[34 + zr], gr.at[0], me)

    @pl.when(edge)
    def _():
        for t in range(8):
            left(kf.at[0, x, y, :, cs], gs.at[24 + t], gr.at[0], me)

    for u in range(2):
        for n in range(2):
            left(far.at[u, n], ss.at[u * 2 + n], rs.at[0], me)
            for d in range(3):
                left(r1.at[u, n, d], ss.at[4 + (u * 2 + n) * 3 + d], rs.at[0], me)
                left(r2.at[u, n, d], ss.at[16 + (u * 2 + n) * 3 + d], rs.at[0], me)
    pl.semaphore_wait(both, 1)
    send4(0)
    kt[...] = jnp.transpose(kf[...].reshape(512, 1024))
    rows_out(ds, kt, do, SCALE)
    dq_out = pltpu.make_async_copy(do, dq, ls.at[1])
    dq_out.start()
    send4(1)
    for u in range(2):
        for zr in range(2):
            for j in range(4):
                def done(u=u, zr=zr, j=j):
                    left(p2.at[u, zr, j], ss.at[28 + u * 8 + zr * 4 + j], rs.at[0], me)

                if zr == 0:
                    pl.when(zl != 2 + j)(done)
                else:
                    done()
    finish(0, out_v)
    finish(1, out_k)
    att_out.wait()
    dq_out.wait()

    @pl.when(owner)
    def _():
        for u in range(2):
            for c in range(2):
                for t in range(8):
                    @pl.when(jnp.logical_or(core != c, zl != t))
                    def _(u=u, c=c, t=t):
                        left(fin.at[0, 0, 0], ss.at[44 + u * 16 + c * 8 + t], rs.at[0], me)


def copy_kernel(*refs):
    given, made, held, sem_in, sem_out = refs[:5], refs[5:10], refs[10:15], refs[15], refs[16]
    ins = [pltpu.make_async_copy(given[i], held[i], sem_in.at[i]) for i in range(5)]
    outs = [pltpu.make_async_copy(held[i], made[i], sem_out.at[i]) for i in range(5)]
    for c in ins:
        c.start()
    for i in range(5):
        ins[i].wait()
        outs[i].start()
    for c in outs:
        c.wait()


def local(queries, experts, gate, prefix_keys, prefix_values, d_out, lengths):
    rows = jax.ShapeDtypeStruct((ROWS, TOPK * HEAD), BF16)
    owned = jax.ShapeDtypeStruct((16, 1024), F32)
    HBM = pl.BlockSpec(memory_space=pltpu.HBM)
    full = pltpu.VMEM((2, 4, 4, 16, 1024), BF16)
    att, dq, ggT, key_grad, value_grad = pl.pallas_call(
        kernel,
        out_shape=(rows, rows, jax.ShapeDtypeStruct((TOPK, ROWS), F32), owned, owned),
        in_specs=[HBM] * 7,
        out_specs=(HBM, HBM, VMEM, VMEM, VMEM),
        scratch_shapes=[
            pltpu.SMEM((64,), jnp.int32),
            pltpu.VMEM((TOPK, ROWS), jnp.int32),
            pltpu.VMEM((TOPK, ROWS), F32),
            pltpu.VMEM((ROWS, 2048), BF16),
            pltpu.VMEM((ROWS, 2048), BF16),
            full,
            full,
            pltpu.VMEM((2048, 1024), BF16),
            pltpu.VMEM((2048, 1024), BF16),
            pltpu.VMEM((256, 2048), F32),
            pltpu.VMEM((256, 2048), F32),
            pltpu.VMEM((512, 2048), BF16),
            pltpu.VMEM((512, 2048), BF16),
            pltpu.VMEM((1024, 512), BF16),
            pltpu.VMEM((1024, 512), BF16),
            pltpu.VMEM((2, 2, 2, 4, 4, 16, 256), BF16),
            pltpu.VMEM((2, 4, 4, 16, 256), F32),
            pltpu.VMEM((2, 2, 2, 4, 4, 16, 256), BF16),
            pltpu.VMEM((2, 2, 2, 4, 4, 16, 256), BF16),
            pltpu.VMEM((2, 2, 3, 2, 4, 16, 256), BF16),
            pltpu.VMEM((2, 2, 2, 4, 16, 256), BF16),
            pltpu.VMEM((2, 2, 3, 2, 16, 256), BF16),
            pltpu.VMEM((2, 2, 4, 16, 128), BF16),
            pltpu.VMEM((2, 2, 8, 16, 128), BF16),
            pltpu.VMEM((2, 2, 4, 16, 128), BF16),
            pltpu.SemaphoreType.DMA((7,)),
            pltpu.SemaphoreType.DMA((36,)),
            pltpu.SemaphoreType.DMA((36,)),
            pltpu.SemaphoreType.DMA((76,)),
            pltpu.SemaphoreType.DMA((76,)),
            pltpu.SemaphoreType.REGULAR,
            pltpu.SemaphoreType.REGULAR,
        ],
        compiler_params=pltpu.CompilerParams(collective_id=0, has_side_effects=True, vmem_limit_bytes=60 << 20),
        name="prefix",
    )(lengths, experts.T, gate.T, queries, d_out, prefix_keys, prefix_values)
    made = (att, dq, ggT, key_grad, value_grad)
    att, dq, ggT, key_grad, value_grad = pl.pallas_call(
        copy_kernel,
        out_shape=tuple(jax.ShapeDtypeStruct(a.shape, a.dtype) for a in made),
        in_specs=[HBM] * 5,
        out_specs=(HBM,) * 5,
        scratch_shapes=[pltpu.VMEM(a.shape, a.dtype) for a in made] + [pltpu.SemaphoreType.DMA((5,))] * 2,
        compiler_params=pltpu.CompilerParams(vmem_limit_bytes=60 << 20),
        name="results",
    )(*made)
    return att, dq, ggT.T, key_grad, value_grad


def solution(mesh):
    torus = Mesh(mesh.devices.reshape(8, 2, 4, 2, 4), AXES)
    in_specs = (P(AXES, None), P(AXES, None), P(AXES, None), P(CTX, None), P(CTX, None), P(AXES, None), P())
    out_specs = (P(AXES, None), P(AXES, None), P(AXES, None), P(CTX, None), P(CTX, None))
    return jax.shard_map(local, mesh=torus, in_specs=in_specs, out_specs=out_specs, check_vma=False)
```

```python
import functools
import math

import jax
import jax.numpy as jnp
from jax import lax
from jax.experimental import pallas as pl
from jax.experimental.pallas import tpu as pltpu
from jax.sharding import Mesh
from jax.sharding import PartitionSpec as P

HEAD = 128
KV_HEADS = 8
TOPK = 16
CLEN = 1024
ROWS = 128
AXES = ("zl", "core", "x", "zh", "y")
CTX = ("x", "zh", "y")
NT = (((1,), (1,)), ((), ()))
NN = (((1,), (0,)), ((), ()))
SCALE = HEAD ** (-0.5)
LOG2E = math.log2(math.e)
F32 = jnp.float32
BF16 = jnp.bfloat16
MESH = pl.DeviceIdType.MESH
VMEM = pl.BlockSpec(memory_space=pltpu.VMEM)
SMEM = pl.BlockSpec(memory_space=pltpu.SMEM)


def place():
    return tuple(lax.axis_index(a) for a in AXES)


def push(src, dst, send, recv, to):
    copy = pltpu.make_async_remote_copy(
        src_ref=src, dst_ref=dst, send_sem=send, recv_sem=recv, device_id=to, device_id_type=MESH
    )
    copy.start()
    return copy


def landed(ref, send, recv, me):
    pltpu.make_async_remote_copy(
        src_ref=ref, dst_ref=ref, send_sem=send, recv_sem=recv, device_id=me, device_id_type=MESH
    ).wait_recv()


def left(ref, send, recv, me):
    pltpu.make_async_remote_copy(
        src_ref=ref, dst_ref=ref, send_sem=send, recv_sem=recv, device_id=me, device_id_type=MESH
    ).wait_send()


def turn(i, d):
    return lax.rem(i + d, 4)


def half(core):
    return pl.ds(pl.multiple_of(core * 512, 512), 512)


def kernel(
    len_in, eT_in, gT_in, q_in, d_in, kp, vp,
    att, dq, ggT, out_k, out_v,
    len_ref, eT, gT, q, do, kf, vf, qx, dx, s0, d0, pf, ds, vt, kt,
    far, near, r0, p0, r1, p1, r2, p2, r3, fin, ls, gs, gr, ss, rs, known, both,
):
    zl, core, x, zh, y = place()
    me = (zl, core, x, zh, y)
    cs, other = half(core), half(1 - core)
    owner, mine_j = jnp.logical_and(zl >= 2, zl < 6), jnp.clip(zl - 2, 0, 3)
    edge = jnp.logical_or(zl == 0, zl == 7)

    loads = [
        pltpu.make_async_copy(kp.at[:, cs], kf.at[0, x, y, :, cs], ls.at[0]),
        pltpu.make_async_copy(vp.at[:, cs], vf.at[0, x, y, :, cs], ls.at[1]),
        pltpu.make_async_copy(eT_in, eT, ls.at[2]),
        pltpu.make_async_copy(gT_in, gT, ls.at[3]),
        pltpu.make_async_copy(q_in, q, ls.at[4]),
        pltpu.make_async_copy(d_in, do, ls.at[5]),
        pltpu.make_async_copy(len_in, len_ref, ls.at[6]),
    ]
    for c in loads:
        c.start()

    def along_z(d):
        z = lax.rem(zh * 8 + zl + d, 16)
        return {"zh": lax.div(z, 8), "zl": lax.rem(z, 8)}

    barrier = pltpu.get_barrier_semaphore()
    for d in (2, 1, 3):
        pl.semaphore_signal(barrier, 1, device_id={"x": turn(x, d)}, device_id_type=MESH)
        pl.semaphore_signal(barrier, 1, device_id={"y": turn(y, d)}, device_id_type=MESH)
    pl.semaphore_signal(barrier, 1, device_id={"core": 1 - core}, device_id_type=MESH)
    for d in (4, 12, 3, 13, 2, 14, 1, 15):
        pl.semaphore_signal(barrier, 1, device_id=along_z(d), device_id_type=MESH)
    pl.semaphore_wait(barrier, 15)

    def gpush(src, dst, at, to):
        push(src, dst, gs.at[at], gr.at[at], to)

    def glanded(ref, at):
        landed(ref, gs.at[at], gr.at[at], me)

    def first(zr):
        for d in (2, 1, 3):
            a, b = zr * 12 + d - 1, zr * 12 + 3 + d - 1
            gpush(kp.at[:, cs] if zr == 0 else kf.at[1, x, y, :, cs], kf.at[zr, x, y, :, cs], a, {"x": turn(x, d)})
            gpush(vp.at[:, cs] if zr == 0 else vf.at[1, x, y, :, cs], vf.at[zr, x, y, :, cs], b, {"y": turn(y, d)})

    def second(zr):
        for d in range(3):
            glanded(kf.at[zr, x, y, :, cs], zr * 12 + d)
        for d in (2, 1, 3):
            gpush(kf.at[zr, :, y, :, cs], kf.at[zr, :, y, :, cs], zr * 12 + 6 + d - 1, {"y": turn(y, d)})
        for d in range(3):
            glanded(vf.at[zr, x, y, :, cs], zr * 12 + 3 + d)
        for d in (2, 1, 3):
            gpush(vf.at[zr, x, :, :, cs], vf.at[zr, x, :, :, cs], zr * 12 + 9 + d - 1, {"x": turn(x, d)})

    def third(zr):
        for d in range(3):
            glanded(kf.at[zr, :, y, :, cs], zr * 12 + 6 + d)
        gpush(kf.at[zr, :, :, :, cs], kf.at[zr, :, :, :, cs], 32 + zr, {"core": 1 - core})
        for d in range(3):
            glanded(vf.at[zr, x, :, :, cs], zr * 12 + 9 + d)
        gpush(vf.at[zr, :, :, :, cs], vf.at[zr, :, :, :, cs], 34 + zr, {"core": 1 - core})

    def swapped(zr):
        glanded(kf.at[zr, :, :, :, other], 32 + zr)
        glanded(vf.at[zr, :, :, :, other], 34 + zr)

    @pl.when(edge)
    def _():
        for t in range(4):
            to = {"zh": 1 - zh, "zl": jnp.where(zl == 0, 4 + t, 3 - t)}
            push(kp.at[:, cs], kf.at[1, x, y, :, cs], gs.at[24 + t], gr.at[24], to)
            push(vp.at[:, cs], vf.at[1, x, y, :, cs], gs.at[28 + t], gr.at[25], to)

    first(0)
    for d in (4, 12):
        pl.semaphore_signal(known, 1, device_id=along_z(d), device_id_type=MESH)
    for c in loads[2:]:
        c.wait()
    headT = lax.div(eT[...], 8)
    for p in range(TOPK):
        rows = slice(p * 128, (p + 1) * 128)
        hc = jnp.transpose(jnp.broadcast_to(headT[p : p + 1, :].astype(F32), (128, 128)))
        q32 = q[:, rows].astype(F32)
        d32 = do[:, rows].astype(F32)
        for h in range(KV_HEADS):
            mine = hc == float(h)
            cols = slice(h * 128, (h + 1) * 128)
            qx[rows, cols] = jnp.where(mine, q32, 0.0).astype(BF16)
            dx[rows, cols] = jnp.where(mine, d32, 0.0).astype(BF16)
    for c in loads[:2]:
        c.wait()
    second(0)
    glanded(kf.at[1, x, y, :, cs], 24)
    glanded(vf.at[1, x, y, :, cs], 25)
    first(1)
    third(0)
    second(1)
    swapped(0)
    k0, v0 = kf[0].reshape(256, 1024), vf[0].reshape(256, 1024)
    for kk in range(8):
        rows = pl.ds(kk * 256, 256)
        s0[:, rows] = lax.dot_general(k0, qx[rows, :], NT, preferred_element_type=F32)
        d0[:, rows] = lax.dot_general(v0, dx[rows, :], NT, preferred_element_type=F32)
    third(1)
    swapped(1)

    block = ((zl * 2 + core) * 32) + ((x * 2 + zh) * 4 + y)
    per = CLEN // ROWS
    length = len_ref[lax.div(block, per)]
    token = lax.broadcasted_iota(jnp.int32, (1, ROWS), 1) + lax.rem(block, per) * ROWS
    live = (token < length).astype(F32)
    lv = jnp.concatenate([live, live], axis=1)
    k1, v1 = kf[1].reshape(256, 1024), vf[1].reshape(256, 1024)
    for kk in range(8):
        rows = pl.ds(kk * 256, 256)
        s = jnp.concatenate(
            [s0[:, rows], lax.dot_general(k1, qx[rows, :], NT, preferred_element_type=F32)], axis=0
        )
        dp = jnp.concatenate(
            [d0[:, rows], lax.dot_general(v1, dx[rows, :], NT, preferred_element_type=F32)], axis=0
        )
        m = jnp.max(s, axis=0, keepdims=True)
        e = jnp.exp2((s - m) * (SCALE * LOG2E))
        inv = 1.0 / jnp.sum(e, axis=0, keepdims=True)
        g = jnp.sum(e * dp, axis=0, keepdims=True) * inv
        gate = jnp.concatenate([gT[2 * kk : 2 * kk + 1, :], gT[2 * kk + 1 : 2 * kk + 2, :]], axis=1)
        w = e * (gate * lv * inv)
        pf[:, rows] = w.astype(BF16)
        ds[:, rows] = (w * (dp - g)).astype(BF16)
        gg = g * lv
        ggT[2 * kk : 2 * kk + 1, :] = gg[:, :128]
        ggT[2 * kk + 1 : 2 * kk + 2, :] = gg[:, 128:]

    def product(u, base, n):
        left_side, right_side = ((pf, dx), (ds, qx))[u]
        cols = pl.ds(pl.multiple_of(base * 512 + n * 256, 256), 256)
        made = lax.dot_general(left_side[...], right_side[:, cols], NN, preferred_element_type=F32)
        if u == 1:
            made = made * SCALE
        return made.reshape(2, 4, 4, 16, 256)

    def send0(u, n):
        far[u, n] = product(u, 1 - core, n).astype(BF16)
        at = u * 2 + n
        push(far.at[u, n], r0.at[u, n], ss.at[at], rs.at[at], {"core": 1 - core})

    def send1(u, n):
        near[...] = product(u, core, n)
        at = u * 2 + n
        landed(r0.at[u, n], ss.at[at], rs.at[at], me)
        p0[u, n] = (near[...] + r0[u, n].astype(F32)).astype(BF16)
        for d in (2, 1, 3):
            at = 4 + (u * 2 + n) * 3 + d - 1
            if n == 0:
                xp = turn(x, d)
                push(p0.at[u, n, :, xp], r1.at[u, n, d - 1], ss.at[at], rs.at[4 + u * 2 + n], {"x": xp})
            else:
                yp = turn(y, d)
                push(p0.at[u, n, :, :, yp], r1.at[u, n, d - 1], ss.at[at], rs.at[4 + u * 2 + n], {"y": yp})

    def send2(u):
        for n in range(2):
            landed(r1.at[u, n], ss.at[0], rs.at[4 + u * 2 + n], me)
            own = p0[u, n, :, x] if n == 0 else p0[u, n, :, :, y]
            acc = own.astype(F32)
            for d in range(3):
                acc = acc + r1[u, n, d].astype(F32)
            p1[u, n] = acc.astype(BF16)
            for d in (2, 1, 3):
                at = 16 + (u * 2 + n) * 3 + d - 1
                if n == 0:
                    yp = turn(y, d)
                    push(p1.at[u, n, :, yp], r2.at[u, n, d - 1], ss.at[at], rs.at[8 + u * 2 + n], {"y": yp})
                else:
                    xp = turn(x, d)
                    push(p1.at[u, n, :, xp], r2.at[u, n, d - 1], ss.at[at], rs.at[8 + u * 2 + n], {"x": xp})

    def send3(u):
        for n in range(2):
            landed(r2.at[u, n], ss.at[0], rs.at[8 + u * 2 + n], me)
            own = p1[u, n, :, y] if n == 0 else p1[u, n, :, x]
            acc = own.astype(F32)
            for d in range(3):
                acc = acc + r2[u, n, d].astype(F32)
            for j in range(2):
                p2[u, :, 2 * n + j] = acc[:, :, j * 128 : (j + 1) * 128].astype(BF16)
        for zr in (1, 0):
            zt = zh if zr == 0 else 1 - zh
            for j in range(4):
                at = 28 + u * 8 + zr * 4 + j

                def go(zr=zr, zt=zt, j=j, at=at):
                    there = rs.at[28 + u * 16 + zl] if zr == 0 else rs.at[36 + u * 16]
                    push(p2.at[u, zr, j], r3.at[u, zr, zl], ss.at[at], there, {"zh": zt, "zl": 2 + j})

                if zr == 0:
                    pl.when(zl != 2 + j)(go)
                else:
                    go()

    def send4():
        @pl.when(owner)
        def _():
            for u in range(2):
                for t in range(8):
                    @pl.when(zl != t)
                    def _(u=u, t=t):
                        landed(r3.at[u, 0, t], ss.at[0], rs.at[28 + u * 16 + t], me)

                landed(r3.at[u, 1], ss.at[0], rs.at[36 + u * 16], me)
                r3[u, 0, zl] = p2[u, 0, mine_j]
                acc = r3[u, 0, 0].astype(F32)
                for i in range(1, 16):
                    acc = acc + r3[u, i // 8, i % 8].astype(F32)
                fin[core, mine_j, u] = acc.astype(BF16)
            tile = fin.at[core, mine_j]
            for t in (7, 0, 6, 1, 5, 2, 4, 3):
                for c in range(2):
                    def go(c=c, t=t):
                        push(tile, tile, ss.at[44 + c * 8 + t], rs.at[60 + core * 4 + mine_j], {"core": c, "zl": t})

                    pl.when(jnp.logical_or(core != c, zl != t))(go)

    def finish():
        for j in (1, 2, 0, 3):
            for c in range(2):
                @pl.when(jnp.logical_or(core != c, zl != 2 + j))
                def _(c=c, j=j):
                    landed(fin.at[c, j], ss.at[0], rs.at[60 + c * 4 + j], me)

                cols = slice((c * 4 + j) * 128, (c * 4 + j + 1) * 128)
                out_v[:, cols] = fin[c, j, 0].astype(F32)
                out_k[:, cols] = fin[c, j, 1].astype(F32)

    def rows_out(src, mat, out, by):
        for kk in range(8):
            hd = jnp.concatenate([headT[2 * kk : 2 * kk + 1, :], headT[2 * kk + 1 : 2 * kk + 2, :]], axis=1)
            full = lax.dot_general(mat[...], src[:, kk * 256 : (kk + 1) * 256], NN, preferred_element_type=F32)
            acc = full[:128, :]
            for h in range(1, KV_HEADS):
                acc = jnp.where(hd == h, full[h * 128 : (h + 1) * 128, :], acc)
            acc = acc * by
            for j in range(2):
                at = (2 * kk + j) * 128
                out[:, at : at + 128] = jnp.transpose(acc[:, j * 128 : (j + 1) * 128]).astype(BF16)

    send0(0, 0)
    send0(0, 1)
    send0(1, 0)
    send1(0, 0)
    send1(0, 1)
    send0(1, 1)
    send1(1, 0)
    send1(1, 1)
    send2(0)
    send2(1)
    pl.semaphore_wait(known, 2)
    pl.semaphore_signal(both, 1, device_id={"core": 1 - core}, device_id_type=MESH)
    send3(0)
    send3(1)
    vt[...] = jnp.transpose(vf[...].reshape(512, 1024))
    rows_out(pf, vt, q, 1.0)
    att_out = pltpu.make_async_copy(q, att, ls.at[0])
    att_out.start()
    kt[...] = jnp.transpose(kf[...].reshape(512, 1024))
    rows_out(ds, kt, do, SCALE)
    dq_out = pltpu.make_async_copy(do, dq, ls.at[1])
    dq_out.start()
    for zr in range(2):
        for d in range(3):
            left(kf.at[zr, x, y, :, cs], gs.at[zr * 12 + d], gr.at[0], me)
            left(vf.at[zr, x, y, :, cs], gs.at[zr * 12 + 3 + d], gr.at[0], me)
            left(kf.at[zr, :, y, :, cs], gs.at[zr * 12 + 6 + d], gr.at[0], me)
            left(vf.at[zr, x, :, :, cs], gs.at[zr * 12 + 9 + d], gr.at[0], me)
        left(kf.at[zr, :, :, :, cs], gs.at[32 + zr], gr.at[0], me)
        left(vf.at[zr, :, :, :, cs], gs.at[34 + zr], gr.at[0], me)

    @pl.when(edge)
    def _():
        for t in range(8):
            left(kf.at[0, x, y, :, cs], gs.at[24 + t], gr.at[0], me)

    for u in range(2):
        for n in range(2):
            left(far.at[u, n], ss.at[u * 2 + n], rs.at[0], me)
            for d in range(3):
                left(r1.at[u, n, d], ss.at[4 + (u * 2 + n) * 3 + d], rs.at[0], me)
                left(r2.at[u, n, d], ss.at[16 + (u * 2 + n) * 3 + d], rs.at[0], me)
    pl.semaphore_wait(both, 1)
    send4()
    for u in range(2):
        for zr in range(2):
            for j in range(4):
                def done(u=u, zr=zr, j=j):
                    left(p2.at[u, zr, j], ss.at[28 + u * 8 + zr * 4 + j], rs.at[0], me)

                if zr == 0:
                    pl.when(zl != 2 + j)(done)
                else:
                    done()
    finish()
    att_out.wait()
    dq_out.wait()

    @pl.when(owner)
    def _():
        for c in range(2):
            for t in range(8):
                @pl.when(jnp.logical_or(core != c, zl != t))
                def _(c=c, t=t):
                    left(fin.at[0, 0], ss.at[44 + c * 8 + t], rs.at[0], me)


def copy_kernel(*refs):
    given, made, held, sem_in, sem_out = refs[:5], refs[5:10], refs[10:15], refs[15], refs[16]
    ins = [pltpu.make_async_copy(given[i], held[i], sem_in.at[i]) for i in range(5)]
    outs = [pltpu.make_async_copy(held[i], made[i], sem_out.at[i]) for i in range(5)]
    for c in ins:
        c.start()
    for i in range(5):
        ins[i].wait()
        outs[i].start()
    for c in outs:
        c.wait()


def local(queries, experts, gate, prefix_keys, prefix_values, d_out, lengths):
    rows = jax.ShapeDtypeStruct((ROWS, TOPK * HEAD), BF16)
    owned = jax.ShapeDtypeStruct((16, 1024), F32)
    HBM = pl.BlockSpec(memory_space=pltpu.HBM)
    full = pltpu.VMEM((2, 4, 4, 16, 1024), BF16)
    att, dq, ggT, key_grad, value_grad = pl.pallas_call(
        kernel,
        out_shape=(rows, rows, jax.ShapeDtypeStruct((TOPK, ROWS), F32), owned, owned),
        in_specs=[HBM] * 7,
        out_specs=(HBM, HBM, VMEM, VMEM, VMEM),
        scratch_shapes=[
            pltpu.SMEM((64,), jnp.int32),
            pltpu.VMEM((TOPK, ROWS), jnp.int32),
            pltpu.VMEM((TOPK, ROWS), F32),
            pltpu.VMEM((ROWS, 2048), BF16),
            pltpu.VMEM((ROWS, 2048), BF16),
            full,
            full,
            pltpu.VMEM((2048, 1024), BF16),
            pltpu.VMEM((2048, 1024), BF16),
            pltpu.VMEM((256, 2048), F32),
            pltpu.VMEM((256, 2048), F32),
            pltpu.VMEM((512, 2048), BF16),
            pltpu.VMEM((512, 2048), BF16),
            pltpu.VMEM((1024, 512), BF16),
            pltpu.VMEM((1024, 512), BF16),
            pltpu.VMEM((2, 2, 2, 4, 4, 16, 256), BF16),
            pltpu.VMEM((2, 4, 4, 16, 256), F32),
            pltpu.VMEM((2, 2, 2, 4, 4, 16, 256), BF16),
            pltpu.VMEM((2, 2, 2, 4, 4, 16, 256), BF16),
            pltpu.VMEM((2, 2, 3, 2, 4, 16, 256), BF16),
            pltpu.VMEM((2, 2, 2, 4, 16, 256), BF16),
            pltpu.VMEM((2, 2, 3, 2, 16, 256), BF16),
            pltpu.VMEM((2, 2, 4, 16, 128), BF16),
            pltpu.VMEM((2, 2, 8, 16, 128), BF16),
            pltpu.VMEM((2, 4, 2, 16, 128), BF16),
            pltpu.SemaphoreType.DMA((7,)),
            pltpu.SemaphoreType.DMA((36,)),
            pltpu.SemaphoreType.DMA((36,)),
            pltpu.SemaphoreType.DMA((76,)),
            pltpu.SemaphoreType.DMA((76,)),
            pltpu.SemaphoreType.REGULAR,
            pltpu.SemaphoreType.REGULAR,
        ],
        compiler_params=pltpu.CompilerParams(collective_id=0, has_side_effects=True, vmem_limit_bytes=60 << 20),
        name="prefix",
    )(lengths, experts.T, gate.T, queries, d_out, prefix_keys, prefix_values)
    made = (att, dq, ggT, key_grad, value_grad)
    att, dq, ggT, key_grad, value_grad = pl.pallas_call(
        copy_kernel,
        out_shape=tuple(jax.ShapeDtypeStruct(a.shape, a.dtype) for a in made),
        in_specs=[HBM] * 5,
        out_specs=(HBM,) * 5,
        scratch_shapes=[pltpu.VMEM(a.shape, a.dtype) for a in made] + [pltpu.SemaphoreType.DMA((5,))] * 2,
        compiler_params=pltpu.CompilerParams(vmem_limit_bytes=60 << 20),
        name="results",
    )(*made)
    return att, dq, ggT.T, key_grad, value_grad


def solution(mesh):
    torus = Mesh(mesh.devices.reshape(8, 2, 4, 2, 4), AXES)
    in_specs = (P(AXES, None), P(AXES, None), P(AXES, None), P(CTX, None), P(CTX, None), P(AXES, None), P())
    out_specs = (P(AXES, None), P(AXES, None), P(AXES, None), P(CTX, None), P(CTX, None))
    return jax.shard_map(local, mesh=torus, in_specs=in_specs, out_specs=out_specs, check_vma=False)
```
